32 devices in a mesh: pts: 4 (over x, core), rows: 8 (over z, y).
Axes of the slice: x: 2, y: 2, z: 4, core: 2. Of those that a mesh axis runs over, the one named last changes fastest.
Arguments:
- solutions: bfloat16 [8, 65536, 128], P('pts', 'rows'), may hold values from -6 to 6
- probe: bfloat16 [64, 65536], P(None, 'rows'), may hold values from -0.0234375 to 0.0234375
- left_factor: float32 [256, 256], replicated, may hold values from -0.375 to 0.375
- singular: float32 [256], replicated, may hold values from 1 to 13.8, as said below
- right_factor: float32 [256, 256], replicated, may hold values from -0.375 to 0.375
- reduced_adjoint: float32 [256, 256], replicated, may hold values from -6 to 6
Outputs:
- solution_adjoint: bfloat16 [8, 65536, 128], P('pts', 'rows')
The draws below stay inside these ranges and needn't reach their ends.
Inputs may be any that keep to these rules, and one draw needn't show every extreme that they name: `singular`: rising, each value at least 0.03 above the one before.
All inputs are finite; a program needn't handle non-finite values.
Results may differ from the reference program's by a relative error of at most 0.0049.
Values sent between devices are 32-bit elements; how exact they have to be, the bound alone decides.
No kernel may reach another device: no remote copies, remote signals or barrier semaphores. Data moves between devices by JAX's collectives and lax.ppermute only.
A program may use at most 64 MiB of HBM per device.

```python
import math
import jax
import jax.numpy as jnp
from jax import lax

L = 64
K = 4
HANK = 256
PTS = 8
N = 65536


def draw_singular(key, part):
    jitter = jax.random.uniform(key, (HANK,), jnp.float32)
    return 1.0 + 0.05 * jnp.arange(HANK, dtype=jnp.float32) + 0.02 * jitter


def shard_levels(key, extent, shards, least, top_value):
    def one(position, shards_of):
        draws = jax.random.uniform(jax.random.fold_in(jax.random.fold_in(key, 6), position), (shards_of,), jnp.float32, least / len(shards), top_value / len(shards))
        return jnp.repeat(jnp.exp(draws), extent[position] // shards_of).reshape((-1,) + (1,) * (len(extent) - position - 1))

    loudness = one(*shards[0])
    for cut in shards[1:]:
        loudness = loudness * one(*cut)
    return loudness


def bell_draw(key, extent, scale, most, split=(), kind=jnp.bfloat16):
    entries = jax.random.normal(key, extent, jnp.float32) * scale
    if len(split) > 0:
        entries = shard_levels(key, extent, split, -0.22, 0.18) * entries
    return jnp.clip(entries, min=-most, max=most).astype(kind)


def setup_inputs(seed: int = 0) -> dict:
    key_of = jax.random.split(jax.random.key(seed), 7)
    return {
        "solutions": bell_draw(key_of[0], (PTS, N, 2 * L), 1.0, 6.0, ((0, 4), (1, 8))),
        "probe": bell_draw(key_of[1], (L, N), N ** -0.5, 0.0234375, ((1, 8),)),
        "left_factor": bell_draw(key_of[2], (HANK, HANK), HANK ** -0.5, 0.375, (), jnp.float32),
        "singular": draw_singular(jax.random.fold_in(key_of[6], 71), 0),
        "right_factor": bell_draw(key_of[4], (HANK, HANK), HANK ** -0.5, 0.375, (), jnp.float32),
        "reduced_adjoint": bell_draw(key_of[5], (HANK, HANK), 1.0, 6.0, (), jnp.float32),
    }


def coefficients(first, count, total, orders):
    theta = math.pi * (first + jnp.arange(count, dtype=jnp.float32) + 0.5) / total
    angle = theta[:, None] * orders[None, :]
    return jnp.cos(angle) / total, jnp.sin(angle) / total


def matmul(first, second):
    return jnp.dot(first, second, precision=lax.Precision.HIGHEST, preferred_element_type=jnp.float32)


def svd_back(hankel, left, sing, right, adjoint):
    quot = matmul(left.T, hankel)
    prod_right = matmul(hankel, right)
    zmat = matmul(quot, right)
    zbar = adjoint / sing[None, :]
    sbar = -jnp.sum(adjoint * zmat, axis=0) / (sing * sing)
    ubar = matmul(prod_right, zbar.T)
    wbar = matmul(quot.T, zbar)
    left_term = matmul(left.T, ubar)
    right_term = matmul(right.T, wbar)
    square = sing * sing
    eye_mask = jnp.eye(sing.shape[0], dtype=bool)
    recip = jnp.where(eye_mask, 0.0, 1.0 / jnp.where(eye_mask, 1.0, square[None, :] - square[:, None]))
    core = (recip * (left_term - left_term.T)) * sing[None, :] + jnp.diag(sbar) + sing[:, None] * (recip * (right_term - right_term.T))
    return core, zbar


def build_hankel(moments):
    return jnp.concatenate([jnp.concatenate([moments[i + j] for j in range(K)], axis=1) for i in range(K)], axis=0)


def reference(solutions, probe, left_factor, singular, right_factor, reduced_adjoint):
    hi = lax.Precision.HIGHEST
    gram = lax.map(lambda sol: jnp.dot(probe, sol, preferred_element_type=jnp.float32), solutions)
    orders = jnp.arange(1, 2 * K + 1, dtype=jnp.float32)
    cos_t, sin_t = coefficients(0.0, PTS, PTS, orders)
    moments = jnp.einsum("pk,plc->klc", cos_t[:, 1:], gram[:, :, :L], precision=hi) - jnp.einsum("pk,plc->klc", sin_t[:, 1:], gram[:, :, L:], precision=hi)
    hankel = build_hankel(moments)
    core, zbar = svd_back(hankel, left_factor, singular, right_factor, reduced_adjoint)
    first_bar = matmul(matmul(left_factor, core), right_factor.T)
    second_bar = matmul(matmul(left_factor, zbar), right_factor.T)
    blocks = [jnp.zeros((L, L), jnp.float32) for k in range(2 * K)]
    for i in range(K):
        for j in range(K):
            blocks[i + j] = blocks[i + j] + first_bar[i * L:(i + 1) * L, j * L:(j + 1) * L]
            blocks[i + j + 1] = blocks[i + j + 1] + second_bar[i * L:(i + 1) * L, j * L:(j + 1) * L]
    moment_adjoint = jnp.stack(blocks)
    weights = jnp.concatenate([jnp.einsum("pk,klc->plc", cos_t, moment_adjoint, precision=hi), -jnp.einsum("pk,klc->plc", sin_t, moment_adjoint, precision=hi)], axis=2).astype(jnp.bfloat16)
    return lax.map(lambda wgt: jnp.dot(probe.T, wgt, preferred_element_type=jnp.float32).astype(jnp.bfloat16), weights)
```

```python
import functools
import math

import jax
import jax.numpy as jnp
import numpy as np
from jax import lax
from jax.experimental import pallas as pl
from jax.experimental.pallas import tpu as pltpu
from jax.sharding import PartitionSpec as P

F32 = jnp.float32
BF16 = jnp.bfloat16
VMEM_BYTES = 50 * 1024 * 1024


def dot(first, second):
    return jnp.dot(first, second, preferred_element_type=F32)


def split(value):
    high = value.astype(BF16)
    return high, (value - high.astype(F32)).astype(BF16)


def left3(value):
    high, low = split(value)
    return jnp.concatenate([high, high, low], axis=1)


def right3(value):
    high, low = split(value)
    return jnp.concatenate([high, low, high], axis=0)


def moment_table(total, blocks, width):
    theta = math.pi * (np.arange(total) + 0.5) / total
    table = np.zeros((total, 2 * blocks, 2 * width), np.float32)
    for a in range(blocks):
        left = 2 * a + 2
        right = left + 1 if a < blocks - 1 else left
        cos_l, sin_l = np.cos(left * theta) / total, np.sin(left * theta) / total
        cos_r, sin_r = np.cos(right * theta) / total, np.sin(right * theta) / total
        table[:, a, :width] = cos_l[:, None]
        table[:, a, width:] = -sin_r[:, None]
        table[:, blocks + a, :width] = -sin_l[:, None]
        table[:, blocks + a, width:] = cos_r[:, None]
    return table


def phase_table(total, blocks):
    theta = math.pi * (np.arange(total)[:, None] + 0.5) / total
    half = theta * (np.arange(blocks + 1)[None, :] + 0.5)
    return np.concatenate([np.cos(half), -np.sin(half)], axis=1).astype(np.float32)


def gram_kernel(chunks, blocks, probe_hbm, sol_hbm, table_ref, keep_ref, send_ref, pbuf, sbuf, psem, ssem):
    count, local, width2 = sbuf.shape
    width = width2 // 2
    size = local // chunks
    me = lax.axis_index("pts")

    def copies(c):
        at = pl.ds(c * size, size)
        return (
            pltpu.make_async_copy(probe_hbm.at[:, at], pbuf.at[:, at], psem.at[c]),
            pltpu.make_async_copy(sol_hbm.at[:, at, :], sbuf.at[:, at, :], ssem.at[c]),
        )

    for c in range(chunks):
        for copy in copies(c):
            copy.start()
    gram = None
    for c in range(chunks):
        for copy in copies(c):
            copy.wait()
        at = pl.ds(c * size, size)
        side = jnp.concatenate([sbuf[p, at, :] for p in range(count)], axis=1)
        part = dot(pbuf[:, at], side)
        gram = part if gram is None else gram + part
    tiles = [None] * blocks
    for p in range(count):
        straight = gram[:, p * width2 : (p + 1) * width2]
        turned = pltpu.roll(straight, width, 1)
        coef = table_ref[me * count + p]
        for a in range(blocks):
            term = straight * coef[a : a + 1] + turned * coef[blocks + a : blocks + a + 1]
            tiles[a] = term if tiles[a] is None else tiles[a] + term
    rows = gram.shape[0] // 2
    lane = lax.broadcasted_iota(jnp.int32, (rows // 2, width2), 1)
    halves = []
    for h in range(2):
        cut = [tile[h * rows : (h + 1) * rows] for tile in tiles]
        last = jnp.where(lane < width, cut[-1][: rows // 2], cut[-1][rows // 2 :])
        halves.append(jnp.concatenate(cut[:-1] + [last], axis=0))
    first = me % 2 == 0
    keep_ref[...] = jnp.where(first, halves[0], halves[1])
    send_ref[...] = jnp.where(first, halves[1], halves[0])


def prep_kernel(
    count,
    blocks,
    left_ref,
    sing_ref,
    right_ref,
    adj_ref,
    phase_ref,
    ut3_ref,
    w3_ref,
    zt3_ref,
    zl3_ref,
    f1_ref,
    f2_ref,
    dg_ref,
    up3_ref,
    wc3_ref,
    y2_ref,
):
    me = lax.axis_index("pts")
    order = left_ref.shape[0]
    width = order // blocks
    left = left_ref[...]
    right = right_ref[...]
    sing = sing_ref[...]
    zbar = adj_ref[...] / sing
    ut3_ref[...] = left3(left.T)
    w3_ref[...] = right3(right)
    zbar_t = zbar.T
    zt3_ref[...] = right3(zbar_t)
    zl3_ref[...] = left3(zbar_t)
    by_column = jnp.broadcast_to(sing, (order, order))
    by_row = by_column.T
    row = lax.broadcasted_iota(jnp.int32, (order, order), 0)
    column = lax.broadcasted_iota(jnp.int32, (order, order), 1)
    eye = row == column
    recip = jnp.where(
        eye, 0.0, 1.0 / jnp.where(eye, 1.0, by_column * by_column - by_row * by_row)
    )
    f1_ref[...] = recip * by_column
    f2_ref[...] = recip * by_row
    dg_ref[...] = jnp.where(eye, -1.0 / by_column, 0.0)
    total = phase_ref.shape[0]
    up, up2 = [], []
    for p in range(count):
        def turn(source, by, sine):
            out = None
            for i in range(blocks):
                term = source[i * width : (i + 1) * width] * phase_ref[
                    me * count + p, sine * (blocks + 1) + by + i
                ]
                out = term if out is None else out + term
            return out

        up += [turn(left, 0, 0) * (1.0 / total), turn(left, 0, 1) * (1.0 / total)]
        up2 += [turn(left, 1, 0) * (1.0 / total), turn(left, 1, 1) * (1.0 / total)]
        wre, wim = turn(right, 0, 0).T, turn(right, 0, 1).T
        wc = jnp.concatenate(
            [jnp.concatenate([wre, wim], axis=1), jnp.concatenate([-wim, wre], axis=1)], axis=0
        )
        wc3_ref[p] = right3(wc)
    up3_ref[...] = left3(jnp.concatenate(up, axis=0))
    y2_ref[...] = dot(left3(jnp.concatenate(up2, axis=0)), right3(zbar))


def turn_kernel(probe_ref, out_ref):
    out_ref[...] = probe_ref[...].T


def post_kernel(
    chunks,
    blocks,
    own_ref,
    got_ref,
    ut3_ref,
    w3_ref,
    zt3_ref,
    zl3_ref,
    f1_ref,
    f2_ref,
    dg_ref,
    up3_ref,
    wc3_ref,
    y2_ref,
    probe_t_ref,
    out_hbm,
    obuf,
    osem,
):
    count, local, width2 = obuf.shape
    width = width2 // 2
    rows = width // 2
    first = lax.axis_index("pts") % 2 == 0
    own, got = own_ref[...], got_ref[...]
    halves = [jnp.where(first, own, got), jnp.where(first, got, own)]
    tiles = [
        jnp.concatenate([half[a * rows : (a + 1) * rows] for half in halves], axis=0)
        for a in range(blocks - 1)
    ]
    packed = [half[(blocks - 1) * rows :] for half in halves]
    last = jnp.concatenate(
        [piece for pack in packed for piece in (pltpu.roll(pack, width, 1), pack)], axis=0
    )
    lane = lax.broadcasted_iota(jnp.int32, (width, width2), 1)
    turned = [pltpu.roll(tile, width, 1) for tile in tiles] + [last]
    between = [jnp.where(lane < width, turned[a], turned[a + 1]) for a in range(blocks - 1)]
    every = [tile for pair in zip(tiles, between) for tile in pair]
    hankel = jnp.concatenate(
        [
            jnp.concatenate([every[i + j] for j in range(0, blocks, 2)], axis=1)
            for i in range(blocks)
        ],
        axis=0,
    )
    quot = dot(ut3_ref[...], right3(hankel))
    zmat = dot(left3(quot), w3_ref[...])
    left_term = dot(left3(zmat), zt3_ref[...])
    right_term = dot(zl3_ref[...], right3(zmat))
    core = (
        f1_ref[...] * (left_term - left_term.T)
        + f2_ref[...] * (right_term.T - right_term)
        + dg_ref[...] * right_term
    )
    prod = dot(up3_ref[...], right3(core)) + y2_ref[...]
    weights = []
    for p in range(count):
        at = 2 * p * width
        pair = jnp.concatenate([prod[at : at + width], prod[at + width : at + 2 * width]], axis=1)
        weights.append(dot(left3(pair), wc3_ref[p]).astype(BF16))
    weights = jnp.concatenate(weights, axis=1)
    size = local // chunks

    def copy(c):
        at = pl.ds(c * size, size)
        return pltpu.make_async_copy(obuf.at[:, at, :], out_hbm.at[:, at, :], osem.at[c])

    for c in range(chunks):
        at = pl.ds(c * size, size)
        part = dot(probe_t_ref[at, :], weights).astype(BF16)
        for p in range(count):
            obuf[p, at, :] = part[:, p * width2 : (p + 1) * width2]
        copy(c).start()
    for c in range(chunks):
        copy(c).wait()


def hop(value, axes, sizes, bits):
    total = math.prod(sizes)
    pairs = []
    for source in range(total):
        place, rest = [], source
        for size in reversed(sizes):
            place.append(rest % size)
            rest //= size
        place = [at ^ bit for at, bit in zip(reversed(place), bits)]
        target = 0
        for size, at in zip(sizes, place):
            target = target * size + at
        pairs.append((source, target))
    return lax.ppermute(value, axes, pairs)


def per_device(n_pts, n_rows, solutions, probe, left_factor, singular, right_factor, adjoint):
    count, local, width2 = solutions.shape
    width = probe.shape[0]
    order = left_factor.shape[0]
    blocks = order // width
    total = count * n_pts
    rows = (blocks - 1) * (width // 2) + width // 4
    chunks = 8 if local % 1024 == 0 else 1
    anyspace = pl.BlockSpec(memory_space=pl.ANY)
    vmem = pl.BlockSpec(memory_space=pltpu.VMEM)
    smem = pl.BlockSpec(memory_space=pltpu.SMEM)
    params = pltpu.CompilerParams(vmem_limit_bytes=VMEM_BYTES)
    half = jax.ShapeDtypeStruct((rows, width2), F32)
    keep, send = pl.pallas_call(
        functools.partial(gram_kernel, chunks, blocks),
        out_shape=(half, half),
        in_specs=[anyspace, anyspace, vmem],
        out_specs=(vmem, vmem),
        scratch_shapes=[
            pltpu.VMEM((width, local), BF16),
            pltpu.VMEM((count, local, width2), BF16),
            pltpu.SemaphoreType.DMA((chunks,)),
            pltpu.SemaphoreType.DMA((chunks,)),
        ],
        compiler_params=params,
        name="gram",
    )(probe, solutions, jnp.asarray(moment_table(total, blocks, width)))

    square = jax.ShapeDtypeStruct((order, order), F32)
    tall = jax.ShapeDtypeStruct((3 * order, order), BF16)
    wide = jax.ShapeDtypeStruct((order, 3 * order), BF16)
    stack = jax.ShapeDtypeStruct((2 * count * width, 3 * order), BF16)
    prep = pl.pallas_call(
        functools.partial(prep_kernel, count, blocks),
        out_shape=(
            wide,
            tall,
            tall,
            wide,
            square,
            square,
            square,
            stack,
            jax.ShapeDtypeStruct((count, 6 * order, width2), BF16),
            jax.ShapeDtypeStruct((2 * count * width, order), F32),
        ),
        in_specs=[vmem, vmem, vmem, vmem, smem],
        out_specs=(vmem,) * 10,
        compiler_params=params,
        cost_estimate=pl.CostEstimate(flops=6 * order**3, bytes_accessed=4 << 20, transcendentals=0),
        name="prep",
    )
    turn = pl.pallas_call(
        turn_kernel,
        out_shape=jax.ShapeDtypeStruct((local, width), BF16),
        in_specs=[vmem],
        out_specs=vmem,
        compiler_params=params,
        cost_estimate=pl.CostEstimate(flops=0, bytes_accessed=6 << 20, transcendentals=0),
        name="turn",
    )
    axes, sizes = ("pts", "rows"), (n_pts, n_rows)
    value = keep + hop(send, axes, sizes, (1, 0))
    phases = jnp.asarray(phase_table(total, blocks))
    value, tied = lax.optimization_barrier((value, (left_factor, singular, right_factor, adjoint)))
    ready = prep(tied[0], tied[1][None, :], tied[2], tied[3], phases)
    hops = [(1 << k, 0) for k in range(1, n_pts.bit_length() - 1)]
    hops += [(0, 1 << k) for k in range(n_rows.bit_length() - 1)]
    for at, bits in enumerate(hops):
        if at == len(hops) - 2:
            value, probe = lax.optimization_barrier((value, probe))
            probe_t = turn(probe)
        value = value + hop(value, axes, sizes, bits)
    other = hop(value, axes, sizes, (1, 0))
    return pl.pallas_call(
        functools.partial(post_kernel, chunks, blocks),
        out_shape=jax.ShapeDtypeStruct((count, local, width2), BF16),
        in_specs=[vmem] * 13,
        out_specs=anyspace,
        scratch_shapes=[
            pltpu.VMEM((count, local, width2), BF16),
            pltpu.SemaphoreType.DMA((chunks,)),
        ],
        compiler_params=params,
        name="post",
    )(value, other, *ready, probe_t)


def solution(mesh):
    in_specs = (P("pts", "rows", None), P(None, "rows"), P(), P(), P(), P())
    out_specs = P("pts", "rows", None)
    return jax.shard_map(
        functools.partial(per_device, mesh.shape["pts"], mesh.shape["rows"]),
        mesh=mesh,
        in_specs=in_specs,
        out_specs=out_specs,
        check_vma=False,
    )
```

```python
import functools
import math

import jax
import jax.numpy as jnp
import numpy as np
from jax import lax
from jax.experimental import pallas as pl
from jax.experimental.pallas import tpu as pltpu
from jax.sharding import PartitionSpec as P

F32 = jnp.float32
BF16 = jnp.bfloat16


def dot(first, second):
    return jnp.dot(first, second, preferred_element_type=F32)


def split(value):
    high = value.astype(BF16)
    return high, (value - high.astype(F32)).astype(BF16)


def left3(value):
    high, low = split(value)
    return jnp.concatenate([high, high, low], axis=1)


def right3(value):
    high, low = split(value)
    return jnp.concatenate([high, low, high], axis=0)


def moment_table(total, blocks, width):
    theta = math.pi * (np.arange(total) + 0.5) / total
    table = np.zeros((total, 2 * blocks, 2 * width), np.float32)
    for a in range(blocks):
        left = 2 * a + 2
        right = left + 1 if a < blocks - 1 else left
        cos_l, sin_l = np.cos(left * theta) / total, np.sin(left * theta) / total
        cos_r, sin_r = np.cos(right * theta) / total, np.sin(right * theta) / total
        table[:, a, :width] = cos_l[:, None]
        table[:, a, width:] = -sin_r[:, None]
        table[:, blocks + a, :width] = -sin_l[:, None]
        table[:, blocks + a, width:] = cos_r[:, None]
    return table


def phase_table(total, blocks):
    theta = math.pi * (np.arange(total)[:, None] + 0.5) / total
    half = theta * (np.arange(blocks + 1)[None, :] + 0.5)
    return np.concatenate([np.cos(half), -np.sin(half)], axis=1).astype(np.float32)


def gram_kernel(
    sizes, blocks, probe_hbm, sol_hbm, table_hbm, keep_ref, send_ref, pbuf, sbuf, table, psem, ssem, tsem
):
    count, local, width2 = sbuf.shape
    width = width2 // 2
    me = lax.axis_index("pts")
    starts = [sum(sizes[:c]) for c in range(len(sizes))]

    def copies(c):
        at = pl.ds(starts[c], sizes[c])
        return (
            pltpu.make_async_copy(probe_hbm.at[:, at], pbuf.at[:, at], psem.at[c]),
            pltpu.make_async_copy(sol_hbm.at[:, at, :], sbuf.at[:, at, :], ssem.at[c]),
        )

    for c in range(len(sizes)):
        for copy in copies(c):
            copy.start()
    fetch = pltpu.make_async_copy(table_hbm.at[pl.ds(me * count, count)], table, tsem)
    fetch.start()
    gram = None
    for c in range(len(sizes)):
        for copy in copies(c):
            copy.wait()
        at = pl.ds(starts[c], sizes[c])
        side = jnp.concatenate([sbuf[p, at, :] for p in range(count)], axis=1)
        part = dot(pbuf[:, at], side)
        gram = part if gram is None else gram + part
    fetch.wait()
    tiles = [None] * blocks
    for p in range(count):
        straight = gram[:, p * width2 : (p + 1) * width2]
        turned = pltpu.roll(straight, width, 1)
        coef = table[p]
        for a in range(blocks):
            term = straight * coef[a : a + 1] + turned * coef[blocks + a : blocks + a + 1]
            tiles[a] = term if tiles[a] is None else tiles[a] + term
    rows = gram.shape[0] // 2
    lane = lax.broadcasted_iota(jnp.int32, (rows // 2, width2), 1)
    halves = []
    for h in range(2):
        cut = [tile[h * rows : (h + 1) * rows] for tile in tiles]
        last = jnp.where(lane < width, cut[-1][: rows // 2], cut[-1][rows // 2 :])
        halves.append(jnp.concatenate(cut[:-1] + [last], axis=0))
    first = me % 2 == 0
    keep_ref[...] = jnp.where(first, halves[0], halves[1])
    send_ref[...] = jnp.where(first, halves[1], halves[0])


def prep_kernel(
    count,
    blocks,
    left_ref,
    sing_ref,
    right_ref,
    adj_ref,
    phase_ref,
    _,
    ut3_ref,
    w3_ref,
    zt3_ref,
    zl3_ref,
    f1_ref,
    f2_ref,
    dg_ref,
    up3_ref,
    wc3_ref,
    y2_ref,
):
    me = lax.axis_index("pts")
    order = left_ref.shape[0]
    width = order // blocks
    left = left_ref[...]
    right = right_ref[...]
    sing = sing_ref[...]
    zbar = adj_ref[...] / sing
    ut3_ref[...] = left3(left.T)
    w3_ref[...] = right3(right)
    zbar_t = zbar.T
    zt3_ref[...] = right3(zbar_t)
    zl3_ref[...] = left3(zbar_t)
    by_column = jnp.broadcast_to(sing, (order, order))
    by_row = by_column.T
    row = lax.broadcasted_iota(jnp.int32, (order, order), 0)
    column = lax.broadcasted_iota(jnp.int32, (order, order), 1)
    eye = row == column
    recip = jnp.where(
        eye, 0.0, 1.0 / jnp.where(eye, 1.0, by_column * by_column - by_row * by_row)
    )
    f1_ref[...] = recip * by_column
    f2_ref[...] = recip * by_row
    dg_ref[...] = jnp.where(eye, -1.0 / by_column, 0.0)
    total = phase_ref.shape[0]
    up, up2 = [], []
    for p in range(count):
        def turn(source, by, sine):
            out = None
            for i in range(blocks):
                term = source[i * width : (i + 1) * width] * phase_ref[
                    me * count + p, sine * (blocks + 1) + by + i
                ]
                out = term if out is None else out + term
            return out

        up += [turn(left, 0, 0) * (1.0 / total), turn(left, 0, 1) * (1.0 / total)]
        up2 += [turn(left, 1, 0) * (1.0 / total), turn(left, 1, 1) * (1.0 / total)]
        wre, wim = turn(right, 0, 0).T, turn(right, 0, 1).T
        wc = jnp.concatenate(
            [jnp.concatenate([wre, wim], axis=1), jnp.concatenate([-wim, wre], axis=1)], axis=0
        )
        wc3_ref[p] = right3(wc)
    up3_ref[...] = left3(jnp.concatenate(up, axis=0))
    y2_ref[...] = dot(left3(jnp.concatenate(up2, axis=0)), right3(zbar))


def sum_kernel(terms, *refs):
    total = refs[0][...]
    for ref in refs[1:terms]:
        total = total + ref[...]
    refs[-1][...] = total


def turn_kernel(probe_ref, _, out_ref):
    out_ref[...] = probe_ref[...].T


def post_kernel(
    chunks,
    blocks,
    own_ref,
    got_ref,
    ut3_ref,
    w3_ref,
    zt3_ref,
    zl3_ref,
    f1_ref,
    f2_ref,
    dg_ref,
    up3_ref,
    wc3_ref,
    y2_ref,
    probe_t_ref,
    out_hbm,
    obuf,
    osem,
):
    count, local, width2 = obuf.shape
    width = width2 // 2
    rows = width // 2
    first = lax.axis_index("pts") % 2 == 0
    own, got = own_ref[...], got_ref[...]
    halves = [jnp.where(first, own, got), jnp.where(first, got, own)]
    tiles = [
        jnp.concatenate([half[a * rows : (a + 1) * rows] for half in halves], axis=0)
        for a in range(blocks - 1)
    ]
    packed = [half[(blocks - 1) * rows :] for half in halves]
    last = jnp.concatenate(
        [piece for pack in packed for piece in (pltpu.roll(pack, width, 1), pack)], axis=0
    )
    lane = lax.broadcasted_iota(jnp.int32, (width, width2), 1)
    turned = [pltpu.roll(tile, width, 1) for tile in tiles] + [last]
    between = [jnp.where(lane < width, turned[a], turned[a + 1]) for a in range(blocks - 1)]
    every = [tile for pair in zip(tiles, between) for tile in pair]
    hankel = jnp.concatenate(
        [
            jnp.concatenate([every[i + j] for j in range(0, blocks, 2)], axis=1)
            for i in range(blocks)
        ],
        axis=0,
    )
    quot = dot(ut3_ref[...], right3(hankel))
    zmat = dot(left3(quot), w3_ref[...])
    left_term = dot(left3(zmat), zt3_ref[...])
    right_term = dot(zl3_ref[...], right3(zmat))
    core = (
        f1_ref[...] * (left_term - left_term.T)
        + f2_ref[...] * (right_term.T - right_term)
        + dg_ref[...] * right_term
    )
    prod = dot(up3_ref[...], right3(core)) + y2_ref[...]
    weights = []
    for p in range(count):
        at = 2 * p * width
        pair = jnp.concatenate([prod[at : at + width], prod[at + width : at + 2 * width]], axis=1)
        weights.append(dot(left3(pair), wc3_ref[p]).astype(BF16))
    weights = jnp.concatenate(weights, axis=1)
    size = local // chunks

    def copy(c):
        at = pl.ds(c * size, size)
        return pltpu.make_async_copy(obuf.at[:, at, :], out_hbm.at[:, at, :], osem.at[c])

    for c in range(chunks):
        at = pl.ds(c * size, size)
        part = dot(probe_t_ref[at, :], weights).astype(BF16)
        for p in range(count):
            obuf[p, at, :] = part[:, p * width2 : (p + 1) * width2]
        copy(c).start()
    for c in range(chunks):
        copy(c).wait()


def hop(value, axes, sizes, bits):
    total = math.prod(sizes)
    pairs = []
    for source in range(total):
        place, rest = [], source
        for size in reversed(sizes):
            place.append(rest % size)
            rest //= size
        place = [at ^ bit for at, bit in zip(reversed(place), bits)]
        target = 0
        for size, at in zip(sizes, place):
            target = target * size + at
        pairs.append((source, target))
    return lax.ppermute(value, axes, pairs)


def per_device(n_pts, n_rows, solutions, probe, left_factor, singular, right_factor, adjoint):
    count, local, width2 = solutions.shape
    width = probe.shape[0]
    order = left_factor.shape[0]
    blocks = order // width
    total = count * n_pts
    rows = (blocks - 1) * (width // 2) + width // 4
    unit = local // 16
    sizes = [unit, unit] + [2 * unit] * 6 + [unit, unit]
    chunks = 8
    anyspace = pl.BlockSpec(memory_space=pl.ANY)
    vmem = pl.BlockSpec(memory_space=pltpu.VMEM)
    smem = pl.BlockSpec(memory_space=pltpu.SMEM)
    params = pltpu.CompilerParams(vmem_limit_bytes=20 << 20)
    in_hbm = functools.partial(pltpu.with_memory_space_constraint, memory_space=pltpu.HBM)
    half = jax.ShapeDtypeStruct((rows, width2), F32)
    keep, send = pl.pallas_call(
        functools.partial(gram_kernel, sizes, blocks),
        out_shape=(half, half),
        in_specs=[anyspace] * 3,
        out_specs=(vmem, vmem),
        scratch_shapes=[
            pltpu.VMEM((width, local), BF16),
            pltpu.VMEM((count, local, width2), BF16),
            pltpu.VMEM((count, 2 * blocks, width2), F32),
            pltpu.SemaphoreType.DMA((len(sizes),)),
            pltpu.SemaphoreType.DMA((len(sizes),)),
            pltpu.SemaphoreType.DMA,
        ],
        compiler_params=params,
        name="gram",
    )(*(in_hbm(v) for v in (probe, solutions, jnp.asarray(moment_table(total, blocks, width)))))

    square = jax.ShapeDtypeStruct((order, order), F32)
    tall = jax.ShapeDtypeStruct((3 * order, order), BF16)
    wide = jax.ShapeDtypeStruct((order, 3 * order), BF16)
    stack = jax.ShapeDtypeStruct((2 * count * width, 3 * order), BF16)
    prep = pl.pallas_call(
        functools.partial(prep_kernel, count, blocks),
        out_shape=(
            wide,
            tall,
            tall,
            wide,
            square,
            square,
            square,
            stack,
            jax.ShapeDtypeStruct((count, 6 * order, width2), BF16),
            jax.ShapeDtypeStruct((2 * count * width, order), F32),
        ),
        in_specs=[vmem, vmem, vmem, vmem, smem, anyspace],
        out_specs=(vmem,) * 10,
        compiler_params=params,
        cost_estimate=pl.CostEstimate(flops=6 * order**3, bytes_accessed=4 << 20, transcendentals=0),
        name="prep",
    )
    turn = pl.pallas_call(
        turn_kernel,
        out_shape=jax.ShapeDtypeStruct((local, width), BF16),
        in_specs=[vmem, anyspace],
        out_specs=vmem,
        compiler_params=params,
        cost_estimate=pl.CostEstimate(flops=0, bytes_accessed=6 << 20, transcendentals=0),
        name="turn",
    )
    axes, sizes_of = ("pts", "rows"), (n_pts, n_rows)
    def add(terms, after):
        return pl.pallas_call(
            functools.partial(sum_kernel, len(terms)),
            out_shape=half,
            in_specs=[vmem] * len(terms) + [anyspace] * len(after),
            out_specs=vmem,
            compiler_params=params,
            name="sum",
        )(*terms, *after)

    value = add([keep, hop(send, axes, sizes_of, (1, 0))], [])
    ready = prep(
        left_factor, singular[None, :], right_factor, adjoint, jnp.asarray(phase_table(total, blocks)), value
    )
    bits = [(1 << k, 0) for k in range(1, n_pts.bit_length() - 1)]
    bits += [(0, 1 << k) for k in range(n_rows.bit_length() - 1)]
    for at in range(0, len(bits), 2):
        step = [tuple(bit) for bit in bits[at : at + 2]]
        if len(step) == 2:
            step.append(tuple(p ^ q for p, q in zip(*step)))
        got = [hop(value, axes, sizes_of, bit) for bit in step]
        if at == 0:
            after = ready
        elif at == 2:
            probe_t = turn(probe, value)
            after = [probe_t]
        else:
            after = []
        value = add([value] + got, after)
    other = hop(value, axes, sizes_of, (1, 0))
    return pl.pallas_call(
        functools.partial(post_kernel, chunks, blocks),
        out_shape=jax.ShapeDtypeStruct((count, local, width2), BF16),
        in_specs=[vmem] * 13,
        out_specs=anyspace,
        scratch_shapes=[
            pltpu.VMEM((count, local, width2), BF16),
            pltpu.SemaphoreType.DMA((chunks,)),
        ],
        compiler_params=params,
        name="post",
    )(value, other, *ready, probe_t)


def solution(mesh):
    in_specs = (P("pts", "rows", None), P(None, "rows"), P(), P(), P(), P())
    out_specs = P("pts", "rows", None)
    return jax.shard_map(
        functools.partial(per_device, mesh.shape["pts"], mesh.shape["rows"]),
        mesh=mesh,
        in_specs=in_specs,
        out_specs=out_specs,
        check_vma=False,
    )
```

```python
import functools
import math

import jax
import jax.numpy as jnp
import numpy as np
from jax import lax
from jax.experimental import pallas as pl
from jax.experimental.pallas import tpu as pltpu
from jax.sharding import PartitionSpec as P

F32 = jnp.float32
BF16 = jnp.bfloat16


def dot(first, second):
    return jnp.dot(first, second, preferred_element_type=F32)


def split(value):
    high = value.astype(BF16)
    return high, (value - high.astype(F32)).astype(BF16)


def left3(value):
    high, low = split(value)
    return jnp.concatenate([high, high, low], axis=1)


def right3(value):
    high, low = split(value)
    return jnp.concatenate([high, low, high], axis=0)


def moment_table(total, blocks, width):
    theta = math.pi * (np.arange(total) + 0.5) / total
    table = np.zeros((total, 2 * blocks, 2 * width), np.float32)
    for a in range(blocks):
        left = 2 * a + 2
        right = left + 1 if a < blocks - 1 else left
        cos_l, sin_l = np.cos(left * theta) / total, np.sin(left * theta) / total
        cos_r, sin_r = np.cos(right * theta) / total, np.sin(right * theta) / total
        table[:, a, :width] = cos_l[:, None]
        table[:, a, width:] = -sin_r[:, None]
        table[:, blocks + a, :width] = -sin_l[:, None]
        table[:, blocks + a, width:] = cos_r[:, None]
    return table


def phase_table(total, blocks):
    theta = math.pi * (np.arange(total)[:, None] + 0.5) / total
    half = theta * (np.arange(blocks + 1)[None, :] + 0.5)
    return np.concatenate([np.cos(half), -np.sin(half)], axis=1).astype(np.float32)


def gram_kernel(sizes, probe_hbm, sol_hbm, out_ref, pbuf, sbuf, psem, ssem):
    count = sbuf.shape[0]
    starts = [sum(sizes[:c]) for c in range(len(sizes))]

    def copies(c):
        at = pl.ds(starts[c], sizes[c])
        return (
            pltpu.make_async_copy(probe_hbm.at[:, at], pbuf.at[:, at], psem.at[c]),
            pltpu.make_async_copy(sol_hbm.at[:, at, :], sbuf.at[:, at, :], ssem.at[c]),
        )

    for c in range(len(sizes)):
        for copy in copies(c):
            copy.start()
    gram = None
    for c in range(len(sizes)):
        for copy in copies(c):
            copy.wait()
        at = pl.ds(starts[c], sizes[c])
        side = jnp.concatenate([sbuf[p, at, :] for p in range(count)], axis=1)
        part = dot(pbuf[:, at], side)
        gram = part if gram is None else gram + part
    out_ref[...] = gram


def prep_kernel(
    count,
    blocks,
    left_ref,
    sing_ref,
    right_ref,
    adj_ref,
    phase_ref,
    _,
    ut3_ref,
    w3_ref,
    zt3_ref,
    zl3_ref,
    f1_ref,
    f2_ref,
    dg_ref,
    up3_ref,
    wc3_ref,
    y2_ref,
):
    me = lax.axis_index("pts")
    order = left_ref.shape[0]
    width = order // blocks
    left = left_ref[...]
    right = right_ref[...]
    sing = sing_ref[...]
    zbar = adj_ref[...] / sing
    ut3_ref[...] = left3(left.T)
    w3_ref[...] = right3(right)
    zbar_t = zbar.T
    zt3_ref[...] = right3(zbar_t)
    zl3_ref[...] = left3(zbar_t)
    by_column = jnp.broadcast_to(sing, (order, order))
    by_row = by_column.T
    row = lax.broadcasted_iota(jnp.int32, (order, order), 0)
    column = lax.broadcasted_iota(jnp.int32, (order, order), 1)
    eye = row == column
    recip = jnp.where(
        eye, 0.0, 1.0 / jnp.where(eye, 1.0, by_column * by_column - by_row * by_row)
    )
    f1_ref[...] = recip * by_column
    f2_ref[...] = recip * by_row
    dg_ref[...] = jnp.where(eye, -1.0 / by_column, 0.0)
    total = phase_ref.shape[0]
    up, up2 = [], []
    for p in range(count):
        def turn(source, by, sine):
            out = None
            for i in range(blocks):
                term = source[i * width : (i + 1) * width] * phase_ref[
                    me * count + p, sine * (blocks + 1) + by + i
                ]
                out = term if out is None else out + term
            return out

        up += [turn(left, 0, 0) * (1.0 / total), turn(left, 0, 1) * (1.0 / total)]
        up2 += [turn(left, 1, 0) * (1.0 / total), turn(left, 1, 1) * (1.0 / total)]
        wre, wim = turn(right, 0, 0).T, turn(right, 0, 1).T
        wc = jnp.concatenate(
            [jnp.concatenate([wre, wim], axis=1), jnp.concatenate([-wim, wre], axis=1)], axis=0
        )
        wc3_ref[p] = right3(wc)
    up3_ref[...] = left3(jnp.concatenate(up, axis=0))
    y2_ref[...] = dot(left3(jnp.concatenate(up2, axis=0)), right3(zbar))


def sum_kernel(terms, *refs):
    total = refs[0][...]
    for ref in refs[1:terms]:
        total = total + ref[...]
    refs[-1][...] = total


def turn_kernel(probe_ref, _, out_ref):
    out_ref[...] = probe_ref[...].T


def hankel_of(grams, places, blocks, table_ref):
    width2 = table_ref.shape[2]
    width = width2 // 2
    tiles = [None] * blocks
    for gram, place in zip(grams, places):
        count = gram.shape[1] // width2
        for p in range(count):
            straight = gram[:, p * width2 : (p + 1) * width2]
            turned = pltpu.roll(straight, width, 1)
            coef = table_ref[place * count + p]
            for a in range(blocks):
                term = straight * coef[a : a + 1] + turned * coef[blocks + a : blocks + a + 1]
                tiles[a] = term if tiles[a] is None else tiles[a] + term
    lane = lax.broadcasted_iota(jnp.int32, (width, width2), 1)
    turned = [pltpu.roll(tile, width, 1) for tile in tiles[:-1]] + [tiles[-1]]
    between = [jnp.where(lane < width, turned[a], turned[a + 1]) for a in range(blocks - 1)]
    every = [tile for pair in zip(tiles, between) for tile in pair]
    return jnp.concatenate(
        [
            jnp.concatenate([every[i + j] for j in range(0, blocks, 2)], axis=1)
            for i in range(blocks)
        ],
        axis=0,
    )


def post_kernel(
    sizes,
    blocks,
    masks,
    table_ref,
    ut3_ref,
    w3_ref,
    zt3_ref,
    zl3_ref,
    f1_ref,
    f2_ref,
    dg_ref,
    up3_ref,
    wc3_ref,
    y2_ref,
    probe_t_ref,
    *refs,
):
    gram_refs, (out_hbm, obuf, osem) = refs[: len(masks)], refs[len(masks) :]
    count, _, width2 = obuf.shape
    width = width2 // 2
    me = lax.axis_index("pts")
    places = [jnp.bitwise_xor(me, mask) for mask in masks]
    hankel = hankel_of([ref[...] for ref in gram_refs], places, blocks, table_ref)
    quot = dot(ut3_ref[...], right3(hankel))
    zmat = dot(left3(quot), w3_ref[...])
    left_term = dot(left3(zmat), zt3_ref[...])
    right_term = dot(zl3_ref[...], right3(zmat))
    core = right3(
        f1_ref[...] * (left_term - left_term.T)
        + f2_ref[...] * (right_term.T - right_term)
        + dg_ref[...] * right_term
    )
    starts = [sum(sizes[:c]) for c in range(len(sizes))]

    def copy(p, c):
        at = pl.ds(starts[c], sizes[c])
        sem = osem.at[p * len(sizes) + c]
        return pltpu.make_async_copy(obuf.at[p, at, :], out_hbm.at[p, at, :], sem)

    prods = []
    for p in range(count):
        at = pl.ds(2 * p * width, 2 * width)
        prods.append(dot(up3_ref[at, :], core) + y2_ref[at, :])
    for p in range(count):
        pair = jnp.concatenate([prods[p][:width], prods[p][width:]], axis=1)
        weights = dot(left3(pair), wc3_ref[p]).astype(BF16)
        for c in range(len(sizes)):
            at = pl.ds(starts[c], sizes[c])
            obuf[p, at, :] = dot(probe_t_ref[at, :], weights).astype(BF16)
            copy(p, c).start()
    for p in range(count):
        for c in range(len(sizes)):
            copy(p, c).wait()


def hop(value, axis, size, mask):
    return lax.ppermute(value, axis, [(at, at ^ mask) for at in range(size)])


def per_device(n_pts, n_rows, solutions, probe, left_factor, singular, right_factor, adjoint):
    count, local, width2 = solutions.shape
    width = probe.shape[0]
    order = left_factor.shape[0]
    blocks = order // width
    total = count * n_pts
    unit = local // 16
    anyspace = pl.BlockSpec(memory_space=pl.ANY)
    vmem = pl.BlockSpec(memory_space=pltpu.VMEM)
    smem = pl.BlockSpec(memory_space=pltpu.SMEM)
    params = pltpu.CompilerParams(vmem_limit_bytes=20 << 20)
    in_hbm = functools.partial(pltpu.with_memory_space_constraint, memory_space=pltpu.HBM)
    sizes_in = [unit, unit] + [2 * unit] * 6 + [unit, unit]
    summed = jax.ShapeDtypeStruct((width, count * width2), F32)
    value = pl.pallas_call(
        functools.partial(gram_kernel, sizes_in),
        out_shape=summed,
        in_specs=[anyspace] * 2,
        out_specs=vmem,
        scratch_shapes=[
            pltpu.VMEM((width, local), BF16),
            pltpu.VMEM((count, local, width2), BF16),
            pltpu.SemaphoreType.DMA((len(sizes_in),)),
            pltpu.SemaphoreType.DMA((len(sizes_in),)),
        ],
        compiler_params=params,
        name="gram",
    )(in_hbm(probe), in_hbm(solutions))

    square = jax.ShapeDtypeStruct((order, order), F32)
    tall = jax.ShapeDtypeStruct((3 * order, order), BF16)
    wide = jax.ShapeDtypeStruct((order, 3 * order), BF16)
    stack = jax.ShapeDtypeStruct((2 * count * width, 3 * order), BF16)
    prep = pl.pallas_call(
        functools.partial(prep_kernel, count, blocks),
        out_shape=(
            wide,
            tall,
            tall,
            wide,
            square,
            square,
            square,
            stack,
            jax.ShapeDtypeStruct((count, 6 * order, width2), BF16),
            jax.ShapeDtypeStruct((2 * count * width, order), F32),
        ),
        in_specs=[vmem, vmem, vmem, vmem, smem, anyspace],
        out_specs=(vmem,) * 10,
        compiler_params=params,
        cost_estimate=pl.CostEstimate(flops=6 * order**3, bytes_accessed=4 << 20, transcendentals=0),
        name="prep",
    )
    turn = pl.pallas_call(
        turn_kernel,
        out_shape=jax.ShapeDtypeStruct((local, width), BF16),
        in_specs=[vmem, anyspace],
        out_specs=vmem,
        compiler_params=params,
        cost_estimate=pl.CostEstimate(flops=0, bytes_accessed=6 << 20, transcendentals=0),
        name="turn",
    )

    def add(terms, after):
        return pl.pallas_call(
            functools.partial(sum_kernel, len(terms)),
            out_shape=summed,
            in_specs=[vmem] * len(terms) + [anyspace] * len(after),
            out_specs=vmem,
            compiler_params=params,
            name="sum",
        )(*terms, *after)

    phases = jnp.asarray(phase_table(total, blocks))
    ready, probe_t = None, None
    bits = [1 << k for k in range(n_rows.bit_length() - 1)]
    for at in range(0, len(bits), 2):
        step = bits[at : at + 2]
        if len(step) == 2:
            step = [step[0], step[0] ^ step[1], step[1]]
        got = [hop(value, "rows", n_rows, bit) for bit in step]
        after = []
        if ready is None:
            ready = prep(left_factor, singular[None, :], right_factor, adjoint, phases, value)
            after = ready
        elif probe_t is None:
            probe_t = turn(probe, value)
            after = [probe_t]
        value = add([value] + got, after)
    masks = [0, n_pts - 1] + list(range(1, n_pts - 1))
    grams = [value] + [hop(value, "pts", n_pts, mask) for mask in masks[1:]]
    sizes_out = [unit, unit] + [2 * unit] + [4 * unit] * 3
    return pl.pallas_call(
        functools.partial(post_kernel, sizes_out, blocks, masks),
        out_shape=jax.ShapeDtypeStruct((count, local, width2), BF16),
        in_specs=[vmem] * (12 + len(masks)),
        out_specs=anyspace,
        scratch_shapes=[
            pltpu.VMEM((count, local, width2), BF16),
            pltpu.SemaphoreType.DMA((count * len(sizes_out),)),
        ],
        compiler_params=params,
        name="post",
    )(jnp.asarray(moment_table(total, blocks, width)), *ready, probe_t, *grams)


def solution(mesh):
    in_specs = (P("pts", "rows", None), P(None, "rows"), P(), P(), P(), P())
    out_specs = P("pts", "rows", None)
    return jax.shard_map(
        functools.partial(per_device, mesh.shape["pts"], mesh.shape["rows"]),
        mesh=mesh,
        in_specs=in_specs,
        out_specs=out_specs,
        check_vma=False,
    )
```

```python
import functools
import math

import jax
import jax.numpy as jnp
import numpy as np
from jax import lax
from jax.experimental import pallas as pl
from jax.experimental.pallas import tpu as pltpu
from jax.sharding import PartitionSpec as P

F32 = jnp.float32
BF16 = jnp.bfloat16


def dot(first, second):
    return jnp.dot(first, second, preferred_element_type=F32)


def split(value):
    high = value.astype(BF16)
    return high, (value - high.astype(F32)).astype(BF16)


def left3(value):
    high, low = split(value)
    return jnp.concatenate([high, high, low], axis=1)


def right3(value):
    high, low = split(value)
    return jnp.concatenate([high, low, high], axis=0)


def moment_table(total, blocks, width):
    theta = math.pi * (np.arange(total) + 0.5) / total
    table = np.zeros((total, 2 * blocks, 2 * width), np.float32)
    for a in range(blocks):
        left = 2 * a + 2
        right = left + 1 if a < blocks - 1 else left
        cos_l, sin_l = np.cos(left * theta) / total, np.sin(left * theta) / total
        cos_r, sin_r = np.cos(right * theta) / total, np.sin(right * theta) / total
        table[:, a, :width] = cos_l[:, None]
        table[:, a, width:] = -sin_r[:, None]
        table[:, blocks + a, :width] = -sin_l[:, None]
        table[:, blocks + a, width:] = cos_r[:, None]
    return table


def phase_table(total, blocks):
    theta = math.pi * (np.arange(total)[:, None] + 0.5) / total
    half = theta * (np.arange(blocks + 1)[None, :] + 0.5)
    return np.concatenate([np.cos(half), -np.sin(half)], axis=1).astype(np.float32)


def gram_kernel(sizes, probe_hbm, sol_hbm, out_ref, pbuf, sbuf, psem, ssem):
    count = sbuf.shape[0]
    starts = [sum(sizes[:c]) for c in range(len(sizes))]

    def copies(c):
        at = pl.ds(starts[c], sizes[c])
        return (
            pltpu.make_async_copy(probe_hbm.at[:, at], pbuf.at[:, at], psem.at[c]),
            pltpu.make_async_copy(sol_hbm.at[:, at, :], sbuf.at[:, at, :], ssem.at[c]),
        )

    for c in range(len(sizes)):
        for copy in copies(c):
            copy.start()
    gram = None
    for c in range(len(sizes)):
        for copy in copies(c):
            copy.wait()
        at = pl.ds(starts[c], sizes[c])
        side = jnp.concatenate([sbuf[p, at, :] for p in range(count)], axis=1)
        part = dot(pbuf[:, at], side)
        gram = part if gram is None else gram + part
    out_ref[...] = gram


def prep_kernel(
    count,
    blocks,
    left_ref,
    sing_ref,
    right_ref,
    adj_ref,
    phase_ref,
    _,
    ut3_ref,
    w3_ref,
    zt3_ref,
    zl3_ref,
    f1_ref,
    f2_ref,
    dg_ref,
    up3_ref,
    wc3_ref,
    y2_ref,
):
    me = lax.axis_index("pts")
    order = left_ref.shape[0]
    width = order // blocks
    left = left_ref[...]
    right = right_ref[...]
    sing = sing_ref[...]
    zbar = adj_ref[...] / sing
    ut3_ref[...] = left3(left.T)
    w3_ref[...] = right3(right)
    zbar_t = zbar.T
    zt3_ref[...] = right3(zbar_t)
    zl3_ref[...] = left3(zbar_t)
    by_column = jnp.broadcast_to(sing, (order, order))
    by_row = by_column.T
    row = lax.broadcasted_iota(jnp.int32, (order, order), 0)
    column = lax.broadcasted_iota(jnp.int32, (order, order), 1)
    eye = row == column
    recip = jnp.where(
        eye, 0.0, 1.0 / jnp.where(eye, 1.0, by_column * by_column - by_row * by_row)
    )
    f1_ref[...] = recip * by_column
    f2_ref[...] = recip * by_row
    dg_ref[...] = jnp.where(eye, -1.0 / by_column, 0.0)
    total = phase_ref.shape[0]
    up, up2 = [], []
    for p in range(count):
        def turn(source, by, sine):
            out = None
            for i in range(blocks):
                term = source[i * width : (i + 1) * width] * phase_ref[
                    me * count + p, sine * (blocks + 1) + by + i
                ]
                out = term if out is None else out + term
            return out

        up += [turn(left, 0, 0) * (1.0 / total), turn(left, 0, 1) * (1.0 / total)]
        up2 += [turn(left, 1, 0) * (1.0 / total), turn(left, 1, 1) * (1.0 / total)]
        wre, wim = turn(right, 0, 0).T, turn(right, 0, 1).T
        wc = jnp.concatenate(
            [jnp.concatenate([wre, wim], axis=1), jnp.concatenate([-wim, wre], axis=1)], axis=0
        )
        wc3_ref[p] = right3(wc)
    up3_ref[...] = left3(jnp.concatenate(up, axis=0))
    y2_ref[...] = dot(left3(jnp.concatenate(up2, axis=0)), right3(zbar))


def sum_kernel(terms, *refs):
    total = refs[0][...]
    for ref in refs[1:terms]:
        total = total + ref[...]
    refs[-1][...] = total


def turn_kernel(probe_ref, _, out_ref):
    out_ref[...] = probe_ref[...].T


def mix_kernel(blocks, masks, table_ref, *refs):
    out_ref = refs[-1]
    width2 = table_ref.shape[2]
    width = width2 // 2
    me = lax.axis_index("pts")
    tiles = [None] * blocks
    for mask, ref in zip(masks, refs[:-1]):
        gram = ref[...]
        count = gram.shape[1] // width2
        for p in range(count):
            straight = gram[:, p * width2 : (p + 1) * width2]
            turned = pltpu.roll(straight, width, 1)
            coef = table_ref[jnp.bitwise_xor(me, mask) * count + p]
            for a in range(blocks):
                term = straight * coef[a : a + 1] + turned * coef[blocks + a : blocks + a + 1]
                tiles[a] = term if tiles[a] is None else tiles[a] + term
    rows = width // 2
    lane = lax.broadcasted_iota(jnp.int32, (rows, width2), 1)
    last = jnp.where(lane < width, tiles[-1][:rows], tiles[-1][rows:])
    out_ref[...] = jnp.concatenate(tiles[:-1] + [last], axis=0)


def hankel_of(moments, blocks):
    width2 = moments.shape[1]
    width = width2 // 2
    tiles = [moments[a * width : (a + 1) * width] for a in range(blocks - 1)]
    packed = moments[(blocks - 1) * width :]
    last = jnp.concatenate([pltpu.roll(packed, width, 1), packed], axis=0)
    lane = lax.broadcasted_iota(jnp.int32, (width, width2), 1)
    turned = [pltpu.roll(tile, width, 1) for tile in tiles] + [last]
    between = [jnp.where(lane < width, turned[a], turned[a + 1]) for a in range(blocks - 1)]
    every = [tile for pair in zip(tiles, between) for tile in pair]
    return jnp.concatenate(
        [
            jnp.concatenate([every[i + j] for j in range(0, blocks, 2)], axis=1)
            for i in range(blocks)
        ],
        axis=0,
    )


def post_kernel(
    sizes,
    blocks,
    own_ref,
    got_ref,
    ut3_ref,
    w3_ref,
    zt3_ref,
    zl3_ref,
    f1_ref,
    f2_ref,
    dg_ref,
    up3_ref,
    wc3_ref,
    y2_ref,
    probe_t_ref,
    out_hbm,
    obuf,
    osem,
):
    count, _, width2 = obuf.shape
    width = width2 // 2
    hankel = hankel_of(own_ref[...] + got_ref[...], blocks)
    quot = dot(ut3_ref[...], right3(hankel))
    zmat = dot(left3(quot), w3_ref[...])
    left_term = dot(left3(zmat), zt3_ref[...])
    right_term = dot(zl3_ref[...], right3(zmat))
    core = right3(
        f1_ref[...] * (left_term - left_term.T)
        + f2_ref[...] * (right_term.T - right_term)
        + dg_ref[...] * right_term
    )
    starts = [sum(sizes[:c]) for c in range(len(sizes))]

    def copy(p, c):
        at = pl.ds(starts[c], sizes[c])
        sem = osem.at[p * len(sizes) + c]
        return pltpu.make_async_copy(obuf.at[p, at, :], out_hbm.at[p, at, :], sem)

    prods = []
    for p in range(count):
        at = pl.ds(2 * p * width, 2 * width)
        prods.append(dot(up3_ref[at, :], core) + y2_ref[at, :])
    for p in range(count):
        pair = jnp.concatenate([prods[p][:width], prods[p][width:]], axis=1)
        weights = dot(left3(pair), wc3_ref[p]).astype(BF16)
        for c in range(len(sizes)):
            at = pl.ds(starts[c], sizes[c])
            obuf[p, at, :] = dot(probe_t_ref[at, :], weights).astype(BF16)
            copy(p, c).start()
    for p in range(count):
        for c in range(len(sizes)):
            copy(p, c).wait()


def hop(value, n_pts, n_rows, mask):
    pairs = [
        (pts * n_rows + row, (pts ^ mask[0]) * n_rows + (row ^ mask[1]))
        for pts in range(n_pts)
        for row in range(n_rows)
    ]
    return lax.ppermute(value, ("pts", "rows"), pairs)


def per_device(n_pts, n_rows, solutions, probe, left_factor, singular, right_factor, adjoint):
    count, local, width2 = solutions.shape
    width = probe.shape[0]
    order = left_factor.shape[0]
    blocks = order // width
    total = count * n_pts
    unit = local // 16
    anyspace = pl.BlockSpec(memory_space=pl.ANY)
    vmem = pl.BlockSpec(memory_space=pltpu.VMEM)
    smem = pl.BlockSpec(memory_space=pltpu.SMEM)
    params = pltpu.CompilerParams(vmem_limit_bytes=20 << 20)
    in_hbm = functools.partial(pltpu.with_memory_space_constraint, memory_space=pltpu.HBM)
    sizes_in = [unit, unit] + [2 * unit] * 6 + [unit, unit]
    summed = jax.ShapeDtypeStruct((width, count * width2), F32)
    value = pl.pallas_call(
        functools.partial(gram_kernel, sizes_in),
        out_shape=summed,
        in_specs=[anyspace] * 2,
        out_specs=vmem,
        scratch_shapes=[
            pltpu.VMEM((width, local), BF16),
            pltpu.VMEM((count, local, width2), BF16),
            pltpu.SemaphoreType.DMA((len(sizes_in),)),
            pltpu.SemaphoreType.DMA((len(sizes_in),)),
        ],
        compiler_params=params,
        name="gram",
    )(in_hbm(probe), in_hbm(solutions))

    square = jax.ShapeDtypeStruct((order, order), F32)
    tall = jax.ShapeDtypeStruct((3 * order, order), BF16)
    wide = jax.ShapeDtypeStruct((order, 3 * order), BF16)
    stack = jax.ShapeDtypeStruct((2 * count * width, 3 * order), BF16)
    prep = pl.pallas_call(
        functools.partial(prep_kernel, count, blocks),
        out_shape=(
            wide,
            tall,
            tall,
            wide,
            square,
            square,
            square,
            stack,
            jax.ShapeDtypeStruct((count, 6 * order, width2), BF16),
            jax.ShapeDtypeStruct((2 * count * width, order), F32),
        ),
        in_specs=[vmem, vmem, vmem, vmem, smem, anyspace],
        out_specs=(vmem,) * 10,
        compiler_params=params,
        cost_estimate=pl.CostEstimate(flops=6 * order**3, bytes_accessed=4 << 20, transcendentals=0),
        name="prep",
    )
    turn = pl.pallas_call(
        turn_kernel,
        out_shape=jax.ShapeDtypeStruct((local, width), BF16),
        in_specs=[vmem, anyspace],
        out_specs=vmem,
        compiler_params=params,
        cost_estimate=pl.CostEstimate(flops=0, bytes_accessed=6 << 20, transcendentals=0),
        name="turn",
    )

    def add(terms, after):
        return pl.pallas_call(
            functools.partial(sum_kernel, len(terms)),
            out_shape=summed,
            in_specs=[vmem] * len(terms) + [anyspace] * len(after),
            out_specs=vmem,
            compiler_params=params,
            name="sum",
        )(*terms, *after)

    phases = jnp.asarray(phase_table(total, blocks))
    ready = None
    bits = [1 << k for k in range(1, n_rows.bit_length() - 1)]
    for at in range(0, len(bits), 2):
        step = bits[at : at + 2]
        if len(step) == 2:
            step = [step[0], step[1], step[0] ^ step[1]]
        got = [hop(value, n_pts, n_rows, (0, bit)) for bit in step]
        after = []
        if ready is None:
            ready = prep(left_factor, singular[None, :], right_factor, adjoint, phases, value)
            after = ready
        value = add([value] + got, after)
    others = [(pts, 0) for pts in range(2, n_pts, 2)]
    if n_rows > 1:
        others = [(1, 1)] + others + [(pts ^ 1, 1) for pts, _ in others]
    grams = [value] + [hop(value, n_pts, n_rows, mask) for mask in others]
    probe_t = turn(probe, value)
    rows = (blocks - 1) * width + width // 2
    moments = pl.pallas_call(
        functools.partial(mix_kernel, blocks, [0] + [mask[0] for mask in others]),
        out_shape=jax.ShapeDtypeStruct((rows, width2), F32),
        in_specs=[vmem] * (1 + len(grams)) + [anyspace],
        out_specs=vmem,
        compiler_params=params,
        name="mix",
    )(jnp.asarray(moment_table(total, blocks, width)), *grams, probe_t)
    other = hop(moments, n_pts, n_rows, (1, 0))
    sizes_out = [unit, unit] + [2 * unit] + [4 * unit] * 3
    return pl.pallas_call(
        functools.partial(post_kernel, sizes_out, blocks),
        out_shape=jax.ShapeDtypeStruct((count, local, width2), BF16),
        in_specs=[vmem] * 13,
        out_specs=anyspace,
        scratch_shapes=[
            pltpu.VMEM((count, local, width2), BF16),
            pltpu.SemaphoreType.DMA((count * len(sizes_out),)),
        ],
        compiler_params=params,
        name="post",
    )(moments, other, *ready, probe_t)


def solution(mesh):
    in_specs = (P("pts", "rows", None), P(None, "rows"), P(), P(), P(), P())
    out_specs = P("pts", "rows", None)
    return jax.shard_map(
        functools.partial(per_device, mesh.shape["pts"], mesh.shape["rows"]),
        mesh=mesh,
        in_specs=in_specs,
        out_specs=out_specs,
        check_vma=False,
    )
```

```python
import functools
import math

import jax
import jax.numpy as jnp
import numpy as np
from jax import lax
from jax.experimental import pallas as pl
from jax.experimental.pallas import tpu as pltpu
from jax.sharding import PartitionSpec as P

F32 = jnp.float32
BF16 = jnp.bfloat16


def dot(first, second):
    return jnp.dot(first, second, preferred_element_type=F32)


def split(value):
    high = value.astype(BF16)
    return high, (value - high.astype(F32)).astype(BF16)


def left3(value):
    high, low = split(value)
    return jnp.concatenate([high, high, low], axis=1)


def right3(value):
    high, low = split(value)
    return jnp.concatenate([high, low, high], axis=0)


def moment_table(total, blocks, width):
    theta = math.pi * (np.arange(total) + 0.5) / total
    table = np.zeros((total, 2 * blocks, 2 * width), np.float32)
    for a in range(blocks):
        left = 2 * a + 2
        right = left + 1 if a < blocks - 1 else left
        cos_l, sin_l = np.cos(left * theta) / total, np.sin(left * theta) / total
        cos_r, sin_r = np.cos(right * theta) / total, np.sin(right * theta) / total
        table[:, a, :width] = cos_l[:, None]
        table[:, a, width:] = -sin_r[:, None]
        table[:, blocks + a, :width] = -sin_l[:, None]
        table[:, blocks + a, width:] = cos_r[:, None]
    return table


def phase_table(total, blocks):
    theta = math.pi * (np.arange(total)[:, None] + 0.5) / total
    half = theta * (np.arange(blocks + 1)[None, :] + 0.5)
    return np.concatenate([np.cos(half), -np.sin(half)], axis=1).astype(np.float32)


def gram_kernel(sizes, probe_hbm, sol_hbm, out_ref, pbuf, sbuf, psem, ssem):
    count = sbuf.shape[0]
    starts = [sum(sizes[:c]) for c in range(len(sizes))]

    def copies(c):
        at = pl.ds(starts[c], sizes[c])
        return (
            pltpu.make_async_copy(probe_hbm.at[:, at], pbuf.at[:, at], psem.at[c]),
            pltpu.make_async_copy(sol_hbm.at[:, at, :], sbuf.at[:, at, :], ssem.at[c]),
        )

    for c in range(len(sizes)):
        for copy in copies(c):
            copy.start()
    gram = None
    for c in range(len(sizes)):
        for copy in copies(c):
            copy.wait()
        at = pl.ds(starts[c], sizes[c])
        side = jnp.concatenate([sbuf[p, at, :] for p in range(count)], axis=1)
        part = dot(pbuf[:, at], side)
        gram = part if gram is None else gram + part
    out_ref[...] = gram


def prep_kernel(
    count,
    blocks,
    left_ref,
    sing_ref,
    right_ref,
    adj_ref,
    phase_ref,
    _,
    ut3_ref,
    w3_ref,
    zt3_ref,
    zl3_ref,
    f1_ref,
    f2_ref,
    dg_ref,
    up3_ref,
    wc3_ref,
    y2_ref,
):
    me = lax.axis_index("pts")
    order = left_ref.shape[0]
    width = order // blocks
    left = left_ref[...]
    right = right_ref[...]
    sing = sing_ref[...]
    zbar = adj_ref[...] / sing
    ut3_ref[...] = left3(left.T)
    w3_ref[...] = right3(right)
    zbar_t = zbar.T
    zt3_ref[...] = right3(zbar_t)
    zl3_ref[...] = left3(zbar_t)
    by_column = jnp.broadcast_to(sing, (order, order))
    by_row = by_column.T
    row = lax.broadcasted_iota(jnp.int32, (order, order), 0)
    column = lax.broadcasted_iota(jnp.int32, (order, order), 1)
    eye = row == column
    recip = jnp.where(
        eye, 0.0, 1.0 / jnp.where(eye, 1.0, by_column * by_column - by_row * by_row)
    )
    f1_ref[...] = recip * by_column
    f2_ref[...] = recip * by_row
    dg_ref[...] = jnp.where(eye, -1.0 / by_column, 0.0)
    total = phase_ref.shape[0]
    up, up2 = [], []
    for p in range(count):
        def turn(source, by, sine):
            out = None
            for i in range(blocks):
                term = source[i * width : (i + 1) * width] * phase_ref[
                    me * count + p, sine * (blocks + 1) + by + i
                ]
                out = term if out is None else out + term
            return out

        up += [turn(left, 0, 0) * (1.0 / total), turn(left, 0, 1) * (1.0 / total)]
        up2 += [turn(left, 1, 0) * (1.0 / total), turn(left, 1, 1) * (1.0 / total)]
        wre, wim = turn(right, 0, 0).T, turn(right, 0, 1).T
        wc = jnp.concatenate(
            [jnp.concatenate([wre, wim], axis=1), jnp.concatenate([-wim, wre], axis=1)], axis=0
        )
        wc3_ref[p] = right3(wc)
    up3_ref[...] = left3(jnp.concatenate(up, axis=0))
    y2_ref[...] = dot(left3(jnp.concatenate(up2, axis=0)), right3(zbar))


def sum_kernel(terms, *refs):
    total = refs[0][...]
    for ref in refs[1:terms]:
        total = total + ref[...]
    refs[-1][...] = total


def turn_kernel(probe_ref, _, out_ref):
    out_ref[...] = probe_ref[...].T


def mix_kernel(blocks, masks, table_ref, *refs):
    out_ref = refs[-1]
    width2 = table_ref.shape[2]
    width = width2 // 2
    me = lax.axis_index("pts")
    tiles = [None] * blocks
    for mask, ref in zip(masks, refs[:-1]):
        gram = ref[...]
        count = gram.shape[1] // width2
        for p in range(count):
            straight = gram[:, p * width2 : (p + 1) * width2]
            turned = pltpu.roll(straight, width, 1)
            coef = table_ref[jnp.bitwise_xor(me, mask) * count + p]
            for a in range(blocks):
                term = straight * coef[a : a + 1] + turned * coef[blocks + a : blocks + a + 1]
                tiles[a] = term if tiles[a] is None else tiles[a] + term
    rows = width // 2
    lane = lax.broadcasted_iota(jnp.int32, (rows, width2), 1)
    last = jnp.where(lane < width, tiles[-1][:rows], tiles[-1][rows:])
    out_ref[...] = jnp.concatenate(tiles[:-1] + [last], axis=0)


def hankel_of(moments, blocks):
    width2 = moments.shape[1]
    width = width2 // 2
    tiles = [moments[a * width : (a + 1) * width] for a in range(blocks - 1)]
    packed = moments[(blocks - 1) * width :]
    last = jnp.concatenate([pltpu.roll(packed, width, 1), packed], axis=0)
    lane = lax.broadcasted_iota(jnp.int32, (width, width2), 1)
    turned = [pltpu.roll(tile, width, 1) for tile in tiles] + [last]
    between = [jnp.where(lane < width, turned[a], turned[a + 1]) for a in range(blocks - 1)]
    every = [tile for pair in zip(tiles, between) for tile in pair]
    return jnp.concatenate(
        [
            jnp.concatenate([every[i + j] for j in range(0, blocks, 2)], axis=1)
            for i in range(blocks)
        ],
        axis=0,
    )


def post_kernel(
    sizes,
    blocks,
    own_ref,
    got_ref,
    ut3_ref,
    w3_ref,
    zt3_ref,
    zl3_ref,
    f1_ref,
    f2_ref,
    dg_ref,
    up3_ref,
    wc3_ref,
    y2_ref,
    probe_t_ref,
    out_hbm,
    obuf,
    osem,
):
    count, _, width2 = obuf.shape
    width = width2 // 2
    hankel = hankel_of(own_ref[...] + got_ref[...], blocks)
    quot = dot(ut3_ref[...], right3(hankel))
    zmat = dot(left3(quot), w3_ref[...])
    left_term = dot(left3(zmat), zt3_ref[...])
    right_term = dot(zl3_ref[...], right3(zmat))
    core = right3(
        f1_ref[...] * (left_term - left_term.T)
        + f2_ref[...] * (right_term.T - right_term)
        + dg_ref[...] * right_term
    )
    starts = [sum(sizes[:c]) for c in range(len(sizes))]

    def copy(p, c):
        at = pl.ds(starts[c], sizes[c])
        sem = osem.at[p * len(sizes) + c]
        return pltpu.make_async_copy(obuf.at[p, at, :], out_hbm.at[p, at, :], sem)

    prods = []
    for p in range(count):
        at = pl.ds(2 * p * width, 2 * width)
        prods.append(dot(up3_ref[at, :], core) + y2_ref[at, :])
    for p in range(count):
        pair = jnp.concatenate([prods[p][:width], prods[p][width:]], axis=1)
        weights = dot(left3(pair), wc3_ref[p]).astype(BF16)
        for c in range(len(sizes)):
            at = pl.ds(starts[c], sizes[c])
            obuf[p, at, :] = dot(probe_t_ref[at, :], weights).astype(BF16)
            copy(p, c).start()
    for p in range(count):
        for c in range(len(sizes)):
            copy(p, c).wait()


def hop(value, n_pts, n_rows, mask):
    pairs = [
        (pts * n_rows + row, (pts ^ mask[0]) * n_rows + (row ^ mask[1]))
        for pts in range(n_pts)
        for row in range(n_rows)
    ]
    return lax.ppermute(value, ("pts", "rows"), pairs)


def per_device(n_pts, n_rows, solutions, probe, left_factor, singular, right_factor, adjoint):
    count, local, width2 = solutions.shape
    width = probe.shape[0]
    order = left_factor.shape[0]
    blocks = order // width
    total = count * n_pts
    unit = local // 16
    anyspace = pl.BlockSpec(memory_space=pl.ANY)
    vmem = pl.BlockSpec(memory_space=pltpu.VMEM)
    smem = pl.BlockSpec(memory_space=pltpu.SMEM)
    params = pltpu.CompilerParams(vmem_limit_bytes=20 << 20)
    in_hbm = functools.partial(pltpu.with_memory_space_constraint, memory_space=pltpu.HBM)
    sizes_in = [unit, unit] + [2 * unit] * 6 + [unit, unit]
    summed = jax.ShapeDtypeStruct((width, count * width2), F32)
    value = pl.pallas_call(
        functools.partial(gram_kernel, sizes_in),
        out_shape=summed,
        in_specs=[anyspace] * 2,
        out_specs=vmem,
        scratch_shapes=[
            pltpu.VMEM((width, local), BF16),
            pltpu.VMEM((count, local, width2), BF16),
            pltpu.SemaphoreType.DMA((len(sizes_in),)),
            pltpu.SemaphoreType.DMA((len(sizes_in),)),
        ],
        compiler_params=params,
        name="gram",
    )(in_hbm(probe), in_hbm(solutions))

    square = jax.ShapeDtypeStruct((order, order), F32)
    tall = jax.ShapeDtypeStruct((3 * order, order), BF16)
    wide = jax.ShapeDtypeStruct((order, 3 * order), BF16)
    stack = jax.ShapeDtypeStruct((2 * count * width, 3 * order), BF16)
    prep = pl.pallas_call(
        functools.partial(prep_kernel, count, blocks),
        out_shape=(
            wide,
            tall,
            tall,
            wide,
            square,
            square,
            square,
            stack,
            jax.ShapeDtypeStruct((count, 6 * order, width2), BF16),
            jax.ShapeDtypeStruct((2 * count * width, order), F32),
        ),
        in_specs=[vmem, vmem, vmem, vmem, smem, anyspace],
        out_specs=(vmem,) * 10,
        compiler_params=params,
        cost_estimate=pl.CostEstimate(flops=6 * order**3, bytes_accessed=4 << 20, transcendentals=0),
        name="prep",
    )
    turn = pl.pallas_call(
        turn_kernel,
        out_shape=jax.ShapeDtypeStruct((local, width), BF16),
        in_specs=[vmem, anyspace],
        out_specs=vmem,
        compiler_params=params,
        cost_estimate=pl.CostEstimate(flops=0, bytes_accessed=6 << 20, transcendentals=0),
        name="turn",
    )

    def add(terms, after):
        return pl.pallas_call(
            functools.partial(sum_kernel, len(terms)),
            out_shape=summed,
            in_specs=[vmem] * len(terms) + [anyspace] * len(after),
            out_specs=vmem,
            compiler_params=params,
            name="sum",
        )(*terms, *after)

    phases = jnp.asarray(phase_table(total, blocks))
    ready = None
    bits = [1 << k for k in range(1, n_rows.bit_length() - 1)]
    for at in range(0, len(bits), 2):
        step = bits[at : at + 2]
        if len(step) == 2:
            step = [step[0], step[0] ^ step[1], step[1]]
        got = [hop(value, n_pts, n_rows, (0, bit)) for bit in step]
        after = []
        if ready is None:
            ready = prep(left_factor, singular[None, :], right_factor, adjoint, phases, value)
            after = ready
        value = add([value] + got, after)
    others = [(pts, 0) for pts in range(2, n_pts, 2)]
    if n_rows > 1:
        others = [(1, 1)] + others + [(pts ^ 1, 1) for pts, _ in others]
    grams = [value] + [hop(value, n_pts, n_rows, mask) for mask in others]
    probe_t = turn(probe, value)
    rows = (blocks - 1) * width + width // 2
    moments = pl.pallas_call(
        functools.partial(mix_kernel, blocks, [0] + [mask[0] for mask in others]),
        out_shape=jax.ShapeDtypeStruct((rows, width2), F32),
        in_specs=[vmem] * (1 + len(grams)) + [anyspace],
        out_specs=vmem,
        compiler_params=params,
        name="mix",
    )(jnp.asarray(moment_table(total, blocks, width)), *grams, probe_t)
    other = hop(moments, n_pts, n_rows, (1, 0))
    sizes_out = [unit, unit] + [2 * unit] + [4 * unit] * 3
    return pl.pallas_call(
        functools.partial(post_kernel, sizes_out, blocks),
        out_shape=jax.ShapeDtypeStruct((count, local, width2), BF16),
        in_specs=[vmem] * 13,
        out_specs=anyspace,
        scratch_shapes=[
            pltpu.VMEM((count, local, width2), BF16),
            pltpu.SemaphoreType.DMA((count * len(sizes_out),)),
        ],
        compiler_params=params,
        name="post",
    )(moments, other, *ready, probe_t)


def solution(mesh):
    in_specs = (P("pts", "rows", None), P(None, "rows"), P(), P(), P(), P())
    out_specs = P("pts", "rows", None)
    return jax.shard_map(
        functools.partial(per_device, mesh.shape["pts"], mesh.shape["rows"]),
        mesh=mesh,
        in_specs=in_specs,
        out_specs=out_specs,
        check_vma=False,
    )
```

```python
import functools
import math

import jax
import jax.numpy as jnp
import numpy as np
from jax import lax
from jax.experimental import pallas as pl
from jax.experimental.pallas import tpu as pltpu
from jax.sharding import PartitionSpec as P

F32 = jnp.float32
BF16 = jnp.bfloat16


def dot(first, second):
    return jnp.dot(first, second, preferred_element_type=F32)


def split(value):
    high = value.astype(BF16)
    return high, (value - high.astype(F32)).astype(BF16)


def left3(value):
    high, low = split(value)
    return jnp.concatenate([high, high, low], axis=1)


def right3(value):
    high, low = split(value)
    return jnp.concatenate([high, low, high], axis=0)


def moment_table(total, blocks, width):
    theta = math.pi * (np.arange(total) + 0.5) / total
    table = np.zeros((total, 2 * blocks, 2 * width), np.float32)
    for a in range(blocks):
        left = 2 * a + 2
        right = left + 1 if a < blocks - 1 else left
        cos_l, sin_l = np.cos(left * theta) / total, np.sin(left * theta) / total
        cos_r, sin_r = np.cos(right * theta) / total, np.sin(right * theta) / total
        table[:, a, :width] = cos_l[:, None]
        table[:, a, width:] = -sin_r[:, None]
        table[:, blocks + a, :width] = -sin_l[:, None]
        table[:, blocks + a, width:] = cos_r[:, None]
    return table


def phase_table(total, blocks):
    theta = math.pi * (np.arange(total)[:, None] + 0.5) / total
    half = theta * (np.arange(blocks + 1)[None, :] + 0.5)
    return np.concatenate([np.cos(half), -np.sin(half)], axis=1).astype(np.float32)


def gram_kernel(sizes, probe_hbm, sol_hbm, out_ref, pbuf, sbuf, psem, ssem):
    count = sbuf.shape[0]
    starts = [sum(sizes[:c]) for c in range(len(sizes))]

    def copies(c):
        at = pl.ds(starts[c], sizes[c])
        return (
            pltpu.make_async_copy(probe_hbm.at[:, at], pbuf.at[:, at], psem.at[c]),
            pltpu.make_async_copy(sol_hbm.at[:, at, :], sbuf.at[:, at, :], ssem.at[c]),
        )

    for c in range(len(sizes)):
        for copy in copies(c):
            copy.start()
    gram = None
    for c in range(len(sizes)):
        for copy in copies(c):
            copy.wait()
        at = pl.ds(starts[c], sizes[c])
        side = jnp.concatenate([sbuf[p, at, :] for p in range(count)], axis=1)
        part = dot(pbuf[:, at], side)
        gram = part if gram is None else gram + part
    out_ref[...] = gram


def prep_kernel(
    count,
    blocks,
    left_hbm,
    sing_hbm,
    right_hbm,
    adj_hbm,
    phase_ref,
    _,
    ut3_ref,
    w3_ref,
    zt3_ref,
    zl3_ref,
    f1_ref,
    f2_ref,
    dg_ref,
    up3_ref,
    wc3_ref,
    y2_ref,
    left_ref,
    sing_ref,
    right_ref,
    adj_ref,
    sem,
):
    me = lax.axis_index("pts")
    order = left_ref.shape[0]
    fetches = [
        pltpu.make_async_copy(source, held, sem.at[at])
        for at, (source, held) in enumerate(
            [(left_hbm, left_ref), (sing_hbm, sing_ref), (right_hbm, right_ref), (adj_hbm, adj_ref)]
        )
    ]
    for fetch in fetches:
        fetch.start()
    for fetch in fetches:
        fetch.wait()
    width = order // blocks
    left = left_ref[...]
    right = right_ref[...]
    sing = sing_ref[...]
    zbar = adj_ref[...] / sing
    ut3_ref[...] = left3(left.T)
    w3_ref[...] = right3(right)
    zbar_t = zbar.T
    zt3_ref[...] = right3(zbar_t)
    zl3_ref[...] = left3(zbar_t)
    by_column = jnp.broadcast_to(sing, (order, order))
    by_row = by_column.T
    row = lax.broadcasted_iota(jnp.int32, (order, order), 0)
    column = lax.broadcasted_iota(jnp.int32, (order, order), 1)
    eye = row == column
    recip = jnp.where(
        eye, 0.0, 1.0 / jnp.where(eye, 1.0, by_column * by_column - by_row * by_row)
    )
    f1_ref[...] = recip * by_column
    f2_ref[...] = recip * by_row
    dg_ref[...] = jnp.where(eye, -1.0 / by_column, 0.0)
    total = phase_ref.shape[0]
    up, up2 = [], []
    for p in range(count):
        def turn(source, by, sine):
            out = None
            for i in range(blocks):
                term = source[i * width : (i + 1) * width] * phase_ref[
                    me * count + p, sine * (blocks + 1) + by + i
                ]
                out = term if out is None else out + term
            return out

        up += [turn(left, 0, 0) * (1.0 / total), turn(left, 0, 1) * (1.0 / total)]
        up2 += [turn(left, 1, 0) * (1.0 / total), turn(left, 1, 1) * (1.0 / total)]
        wre, wim = turn(right, 0, 0).T, turn(right, 0, 1).T
        wc = jnp.concatenate(
            [jnp.concatenate([wre, wim], axis=1), jnp.concatenate([-wim, wre], axis=1)], axis=0
        )
        wc3_ref[p] = right3(wc)
    up3_ref[...] = left3(jnp.concatenate(up, axis=0))
    y2_ref[...] = dot(left3(jnp.concatenate(up2, axis=0)), right3(zbar))


def sum_kernel(terms, *refs):
    total = refs[0][...]
    for ref in refs[1:terms]:
        total = total + ref[...]
    refs[-1][...] = total


def turn_kernel(probe_ref, _, out_ref):
    out_ref[...] = probe_ref[...].T


def mix_kernel(blocks, masks, table_ref, *refs):
    out_ref = refs[-1]
    width2 = table_ref.shape[2]
    width = width2 // 2
    me = lax.axis_index("pts")
    tiles = [None] * blocks
    for mask, ref in zip(masks, refs[:-1]):
        gram = ref[...]
        count = gram.shape[1] // width2
        for p in range(count):
            straight = gram[:, p * width2 : (p + 1) * width2]
            turned = pltpu.roll(straight, width, 1)
            coef = table_ref[jnp.bitwise_xor(me, mask) * count + p]
            for a in range(blocks):
                term = straight * coef[a : a + 1] + turned * coef[blocks + a : blocks + a + 1]
                tiles[a] = term if tiles[a] is None else tiles[a] + term
    rows = width // 2
    lane = lax.broadcasted_iota(jnp.int32, (rows, width2), 1)
    last = jnp.where(lane < width, tiles[-1][:rows], tiles[-1][rows:])
    out_ref[...] = jnp.concatenate(tiles[:-1] + [last], axis=0)


def hankel_of(moments, blocks):
    width2 = moments.shape[1]
    width = width2 // 2
    tiles = [moments[a * width : (a + 1) * width] for a in range(blocks - 1)]
    packed = moments[(blocks - 1) * width :]
    last = jnp.concatenate([pltpu.roll(packed, width, 1), packed], axis=0)
    lane = lax.broadcasted_iota(jnp.int32, (width, width2), 1)
    turned = [pltpu.roll(tile, width, 1) for tile in tiles] + [last]
    between = [jnp.where(lane < width, turned[a], turned[a + 1]) for a in range(blocks - 1)]
    every = [tile for pair in zip(tiles, between) for tile in pair]
    return jnp.concatenate(
        [
            jnp.concatenate([every[i + j] for j in range(0, blocks, 2)], axis=1)
            for i in range(blocks)
        ],
        axis=0,
    )


def post_kernel(
    sizes,
    blocks,
    own_ref,
    got_ref,
    ut3_ref,
    w3_ref,
    zt3_ref,
    zl3_ref,
    f1_ref,
    f2_ref,
    dg_ref,
    up3_ref,
    wc3_ref,
    y2_ref,
    probe_t_ref,
    out_hbm,
    obuf,
    osem,
):
    count, _, width2 = obuf.shape
    width = width2 // 2
    hankel = hankel_of(own_ref[...] + got_ref[...], blocks)
    quot = dot(ut3_ref[...], right3(hankel))
    zmat = dot(left3(quot), w3_ref[...])
    left_term = dot(left3(zmat), zt3_ref[...])
    right_term = dot(zl3_ref[...], right3(zmat))
    core = right3(
        f1_ref[...] * (left_term - left_term.T)
        + f2_ref[...] * (right_term.T - right_term)
        + dg_ref[...] * right_term
    )
    starts = [sum(sizes[:c]) for c in range(len(sizes))]

    def copy(p, c):
        at = pl.ds(starts[c], sizes[c])
        sem = osem.at[p * len(sizes) + c]
        return pltpu.make_async_copy(obuf.at[p, at, :], out_hbm.at[p, at, :], sem)

    prods = []
    for p in range(count):
        at = pl.ds(2 * p * width, 2 * width)
        prods.append(dot(up3_ref[at, :], core) + y2_ref[at, :])
    for p in range(count):
        pair = jnp.concatenate([prods[p][:width], prods[p][width:]], axis=1)
        weights = dot(left3(pair), wc3_ref[p]).astype(BF16)
        for c in range(len(sizes)):
            at = pl.ds(starts[c], sizes[c])
            obuf[p, at, :] = dot(probe_t_ref[at, :], weights).astype(BF16)
            copy(p, c).start()
    for p in range(count):
        for c in range(len(sizes)):
            copy(p, c).wait()


def hop(value, n_pts, n_rows, mask):
    pairs = [
        (pts * n_rows + row, (pts ^ mask[0]) * n_rows + (row ^ mask[1]))
        for pts in range(n_pts)
        for row in range(n_rows)
    ]
    return lax.ppermute(value, ("pts", "rows"), pairs)


def per_device(n_pts, n_rows, solutions, probe, left_factor, singular, right_factor, adjoint):
    count, local, width2 = solutions.shape
    width = probe.shape[0]
    order = left_factor.shape[0]
    blocks = order // width
    total = count * n_pts
    unit = local // 16
    anyspace = pl.BlockSpec(memory_space=pl.ANY)
    vmem = pl.BlockSpec(memory_space=pltpu.VMEM)
    smem = pl.BlockSpec(memory_space=pltpu.SMEM)
    params = pltpu.CompilerParams(vmem_limit_bytes=20 << 20)
    in_hbm = functools.partial(pltpu.with_memory_space_constraint, memory_space=pltpu.HBM)
    sizes_in = [unit, unit] + [2 * unit] * 6 + [unit, unit]
    summed = jax.ShapeDtypeStruct((width, count * width2), F32)
    value, held = pl.pallas_call(
        functools.partial(gram_kernel, sizes_in),
        out_shape=(summed, jax.ShapeDtypeStruct((width, local), BF16)),
        in_specs=[anyspace] * 2,
        out_specs=(vmem, vmem),
        scratch_shapes=[
            pltpu.VMEM((count, local, width2), BF16),
            pltpu.SemaphoreType.DMA((len(sizes_in),)),
            pltpu.SemaphoreType.DMA((len(sizes_in),)),
        ],
        compiler_params=params,
        name="gram",
    )(in_hbm(probe), in_hbm(solutions))

    square = jax.ShapeDtypeStruct((order, order), F32)
    tall = jax.ShapeDtypeStruct((3 * order, order), BF16)
    wide = jax.ShapeDtypeStruct((order, 3 * order), BF16)
    stack = jax.ShapeDtypeStruct((2 * count * width, 3 * order), BF16)
    prep = pl.pallas_call(
        functools.partial(prep_kernel, count, blocks),
        out_shape=(
            wide,
            tall,
            tall,
            wide,
            square,
            square,
            square,
            stack,
            jax.ShapeDtypeStruct((count, 6 * order, width2), BF16),
            jax.ShapeDtypeStruct((2 * count * width, order), F32),
        ),
        in_specs=[anyspace] * 4 + [smem, anyspace],
        out_specs=(vmem,) * 10,
        scratch_shapes=[
            pltpu.VMEM((order, order), F32),
            pltpu.VMEM((1, order), F32),
            pltpu.VMEM((order, order), F32),
            pltpu.VMEM((order, order), F32),
            pltpu.SemaphoreType.DMA((4,)),
        ],
        compiler_params=params,
        cost_estimate=pl.CostEstimate(flops=6 * order**3, bytes_accessed=4 << 20, transcendentals=0),
        name="prep",
    )
    turn = pl.pallas_call(
        turn_kernel,
        out_shape=jax.ShapeDtypeStruct((local, width), BF16),
        in_specs=[vmem, anyspace],
        out_specs=vmem,
        compiler_params=params,
        cost_estimate=pl.CostEstimate(flops=0, bytes_accessed=6 << 20, transcendentals=0),
        name="turn",
    )

    def add(terms, after):
        return pl.pallas_call(
            functools.partial(sum_kernel, len(terms)),
            out_shape=summed,
            in_specs=[vmem] * len(terms) + [anyspace] * len(after),
            out_specs=vmem,
            compiler_params=params,
            name="sum",
        )(*terms, *after)

    phases = jnp.asarray(phase_table(total, blocks))
    ready = None
    bits = [1 << k for k in range(1, n_rows.bit_length() - 1)]
    for at in range(0, len(bits), 2):
        step = bits[at : at + 2]
        if len(step) == 2:
            step = [step[0], step[0] ^ step[1], step[1]]
        got = [hop(value, n_pts, n_rows, (0, bit)) for bit in step]
        after = []
        if ready is None:
            factors = (left_factor, singular[None, :], right_factor, adjoint)
            ready = prep(*(in_hbm(v) for v in factors), phases, value)
            after = ready
        value = add([value] + got, after)
    others = [(pts, 0) for pts in range(2, n_pts, 2)]
    if n_rows > 1:
        others = [(1, 1)] + others + [(pts ^ 1, 1) for pts, _ in others]
    grams = [value] + [hop(value, n_pts, n_rows, mask) for mask in others]
    probe_t = turn(held, value)
    rows = (blocks - 1) * width + width // 2
    moments = pl.pallas_call(
        functools.partial(mix_kernel, blocks, [0] + [mask[0] for mask in others]),
        out_shape=jax.ShapeDtypeStruct((rows, width2), F32),
        in_specs=[vmem] * (1 + len(grams)) + [anyspace],
        out_specs=vmem,
        compiler_params=params,
        name="mix",
    )(jnp.asarray(moment_table(total, blocks, width)), *grams, probe_t)
    other = hop(moments, n_pts, n_rows, (1, 0))
    sizes_out = [unit, unit] + [2 * unit] + [4 * unit] * 3
    return pl.pallas_call(
        functools.partial(post_kernel, sizes_out, blocks),
        out_shape=jax.ShapeDtypeStruct((count, local, width2), BF16),
        in_specs=[vmem] * 13,
        out_specs=anyspace,
        scratch_shapes=[
            pltpu.VMEM((count, local, width2), BF16),
            pltpu.SemaphoreType.DMA((count * len(sizes_out),)),
        ],
        compiler_params=params,
        name="post",
    )(moments, other, *ready, probe_t)


def solution(mesh):
    in_specs = (P("pts", "rows", None), P(None, "rows"), P(), P(), P(), P())
    out_specs = P("pts", "rows", None)
    return jax.shard_map(
        functools.partial(per_device, mesh.shape["pts"], mesh.shape["rows"]),
        mesh=mesh,
        in_specs=in_specs,
        out_specs=out_specs,
        check_vma=False,
    )
```

```python
import functools
import math

import jax
import jax.numpy as jnp
import numpy as np
from jax import lax
from jax.experimental import pallas as pl
from jax.experimental.pallas import tpu as pltpu
from jax.sharding import PartitionSpec as P

F32 = jnp.float32
BF16 = jnp.bfloat16


def dot(first, second):
    return jnp.dot(first, second, preferred_element_type=F32)


def split(value):
    high = value.astype(BF16)
    return high, (value - high.astype(F32)).astype(BF16)


def left3(value):
    high, low = split(value)
    return jnp.concatenate([high, high, low], axis=1)


def right3(value):
    high, low = split(value)
    return jnp.concatenate([high, low, high], axis=0)


def moment_table(total, blocks, width):
    theta = math.pi * (np.arange(total) + 0.5) / total
    table = np.zeros((total, 2 * blocks, 2 * width), np.float32)
    for a in range(blocks):
        left = 2 * a + 2
        right = left + 1 if a < blocks - 1 else left
        cos_l, sin_l = np.cos(left * theta) / total, np.sin(left * theta) / total
        cos_r, sin_r = np.cos(right * theta) / total, np.sin(right * theta) / total
        table[:, a, :width] = cos_l[:, None]
        table[:, a, width:] = -sin_r[:, None]
        table[:, blocks + a, :width] = -sin_l[:, None]
        table[:, blocks + a, width:] = cos_r[:, None]
    return table


def phase_table(total, blocks):
    theta = math.pi * (np.arange(total)[:, None] + 0.5) / total
    half = theta * (np.arange(blocks + 1)[None, :] + 0.5)
    return np.concatenate([np.cos(half), -np.sin(half)], axis=1).astype(np.float32)


def gram_kernel(sizes, probe_hbm, sol_hbm, out_ref, pbuf, sbuf, psem, ssem):
    count = sbuf.shape[0]
    starts = [sum(sizes[:c]) for c in range(len(sizes))]
    step = min(sizes)

    def copies(c):
        at = pl.ds(starts[c], sizes[c])
        return (
            pltpu.make_async_copy(probe_hbm.at[:, at], pbuf.at[:, at], psem.at[c]),
            pltpu.make_async_copy(sol_hbm.at[:, at, :], sbuf.at[:, at, :], ssem.at[c]),
        )

    for c in range(len(sizes)):
        for copy in copies(c):
            copy.start()
    gram = None
    for c in range(len(sizes)):
        for copy in copies(c):
            copy.wait()
        for first in range(starts[c], starts[c] + sizes[c], step):
            at = pl.ds(first, step)
            side = jnp.concatenate([sbuf[p, at, :] for p in range(count)], axis=1)
            part = dot(pbuf[:, at], side)
            gram = part if gram is None else gram + part
    out_ref[...] = gram


def prep_kernel(
    count,
    blocks,
    left_hbm,
    sing_hbm,
    right_hbm,
    adj_hbm,
    phase_ref,
    _,
    ut3_ref,
    w3_ref,
    zt3_ref,
    zl3_ref,
    f1_ref,
    f2_ref,
    dg_ref,
    up3_ref,
    wc3_ref,
    y2_ref,
    left_ref,
    sing_ref,
    right_ref,
    adj_ref,
    sem,
):
    me = lax.axis_index("pts")
    order = left_ref.shape[0]
    fetches = [
        pltpu.make_async_copy(source, held, sem.at[at])
        for at, (source, held) in enumerate(
            [(left_hbm, left_ref), (sing_hbm, sing_ref), (right_hbm, right_ref), (adj_hbm, adj_ref)]
        )
    ]
    for fetch in fetches:
        fetch.start()
    for fetch in fetches:
        fetch.wait()
    width = order // blocks
    left = left_ref[...]
    right = right_ref[...]
    sing = sing_ref[...]
    zbar = adj_ref[...] / sing
    ut3_ref[...] = left3(left.T)
    w3_ref[...] = right3(right)
    zbar_t = zbar.T
    zt3_ref[...] = right3(zbar_t)
    zl3_ref[...] = left3(zbar_t)
    by_column = jnp.broadcast_to(sing, (order, order))
    by_row = by_column.T
    row = lax.broadcasted_iota(jnp.int32, (order, order), 0)
    column = lax.broadcasted_iota(jnp.int32, (order, order), 1)
    eye = row == column
    recip = jnp.where(
        eye, 0.0, 1.0 / jnp.where(eye, 1.0, by_column * by_column - by_row * by_row)
    )
    f1_ref[...] = recip * by_column
    f2_ref[...] = recip * by_row
    dg_ref[...] = jnp.where(eye, -1.0 / by_column, 0.0)
    total = phase_ref.shape[0]
    up, up2 = [], []
    for p in range(count):
        def turn(source, by, sine):
            out = None
            for i in range(blocks):
                term = source[i * width : (i + 1) * width] * phase_ref[
                    me * count + p, sine * (blocks + 1) + by + i
                ]
                out = term if out is None else out + term
            return out

        up += [turn(left, 0, 0) * (1.0 / total), turn(left, 0, 1) * (1.0 / total)]
        up2 += [turn(left, 1, 0) * (1.0 / total), turn(left, 1, 1) * (1.0 / total)]
        wre, wim = turn(right, 0, 0).T, turn(right, 0, 1).T
        wc = jnp.concatenate(
            [jnp.concatenate([wre, wim], axis=1), jnp.concatenate([-wim, wre], axis=1)], axis=0
        )
        wc3_ref[p] = right3(wc)
    up3_ref[...] = left3(jnp.concatenate(up, axis=0))
    y2_ref[...] = dot(left3(jnp.concatenate(up2, axis=0)), right3(zbar))


def sum_kernel(terms, *refs):
    total = refs[0][...]
    for ref in refs[1:terms]:
        total = total + ref[...]
    refs[-1][...] = total


def turn_kernel(probe_ref, _, out_ref):
    out_ref[...] = probe_ref[...].T


def mix_kernel(blocks, masks, table_ref, *refs):
    out_ref = refs[-1]
    width2 = table_ref.shape[2]
    width = width2 // 2
    me = lax.axis_index("pts")
    tiles = [None] * blocks
    for mask, ref in zip(masks, refs[:-1]):
        gram = ref[...]
        count = gram.shape[1] // width2
        for p in range(count):
            straight = gram[:, p * width2 : (p + 1) * width2]
            turned = pltpu.roll(straight, width, 1)
            coef = table_ref[jnp.bitwise_xor(me, mask) * count + p]
            for a in range(blocks):
                term = straight * coef[a : a + 1] + turned * coef[blocks + a : blocks + a + 1]
                tiles[a] = term if tiles[a] is None else tiles[a] + term
    rows = width // 2
    lane = lax.broadcasted_iota(jnp.int32, (rows, width2), 1)
    last = jnp.where(lane < width, tiles[-1][:rows], tiles[-1][rows:])
    out_ref[...] = jnp.concatenate(tiles[:-1] + [last], axis=0)


def hankel_of(moments, blocks):
    width2 = moments.shape[1]
    width = width2 // 2
    tiles = [moments[a * width : (a + 1) * width] for a in range(blocks - 1)]
    packed = moments[(blocks - 1) * width :]
    last = jnp.concatenate([pltpu.roll(packed, width, 1), packed], axis=0)
    lane = lax.broadcasted_iota(jnp.int32, (width, width2), 1)
    turned = [pltpu.roll(tile, width, 1) for tile in tiles] + [last]
    between = [jnp.where(lane < width, turned[a], turned[a + 1]) for a in range(blocks - 1)]
    every = [tile for pair in zip(tiles, between) for tile in pair]
    return jnp.concatenate(
        [
            jnp.concatenate([every[i + j] for j in range(0, blocks, 2)], axis=1)
            for i in range(blocks)
        ],
        axis=0,
    )


def post_kernel(
    sizes,
    blocks,
    own_ref,
    got_ref,
    ut3_ref,
    w3_ref,
    zt3_ref,
    zl3_ref,
    f1_ref,
    f2_ref,
    dg_ref,
    up3_ref,
    wc3_ref,
    y2_ref,
    probe_t_ref,
    out_hbm,
    obuf,
    osem,
):
    count, _, width2 = obuf.shape
    width = width2 // 2
    hankel = hankel_of(own_ref[...] + got_ref[...], blocks)
    quot = dot(ut3_ref[...], right3(hankel))
    zmat = dot(left3(quot), w3_ref[...])
    left_term = dot(left3(zmat), zt3_ref[...])
    right_term = dot(zl3_ref[...], right3(zmat))
    core = right3(
        f1_ref[...] * (left_term - left_term.T)
        + f2_ref[...] * (right_term.T - right_term)
        + dg_ref[...] * right_term
    )
    starts = [sum(sizes[:c]) for c in range(len(sizes))]

    def copy(p, c):
        at = pl.ds(starts[c], sizes[c])
        sem = osem.at[p * len(sizes) + c]
        return pltpu.make_async_copy(obuf.at[p, at, :], out_hbm.at[p, at, :], sem)

    prods = []
    for p in range(count):
        at = pl.ds(2 * p * width, 2 * width)
        prods.append(dot(up3_ref[at, :], core) + y2_ref[at, :])
    for p in range(count):
        pair = jnp.concatenate([prods[p][:width], prods[p][width:]], axis=1)
        weights = dot(left3(pair), wc3_ref[p]).astype(BF16)
        for c in range(len(sizes)):
            at = pl.ds(starts[c], sizes[c])
            obuf[p, at, :] = dot(probe_t_ref[at, :], weights).astype(BF16)
            copy(p, c).start()
    for p in range(count):
        for c in range(len(sizes)):
            copy(p, c).wait()


def hop(value, n_pts, n_rows, mask):
    pairs = [
        (pts * n_rows + row, (pts ^ mask[0]) * n_rows + (row ^ mask[1]))
        for pts in range(n_pts)
        for row in range(n_rows)
    ]
    return lax.ppermute(value, ("pts", "rows"), pairs)


def per_device(n_pts, n_rows, solutions, probe, left_factor, singular, right_factor, adjoint):
    count, local, width2 = solutions.shape
    width = probe.shape[0]
    order = left_factor.shape[0]
    blocks = order // width
    total = count * n_pts
    unit = local // 16
    anyspace = pl.BlockSpec(memory_space=pl.ANY)
    vmem = pl.BlockSpec(memory_space=pltpu.VMEM)
    smem = pl.BlockSpec(memory_space=pltpu.SMEM)
    params = pltpu.CompilerParams(vmem_limit_bytes=20 << 20)
    in_hbm = functools.partial(pltpu.with_memory_space_constraint, memory_space=pltpu.HBM)
    sizes_in = [2 * unit] * 7 + [unit, unit]
    summed = jax.ShapeDtypeStruct((width, count * width2), F32)
    value, held = pl.pallas_call(
        functools.partial(gram_kernel, sizes_in),
        out_shape=(summed, jax.ShapeDtypeStruct((width, local), BF16)),
        in_specs=[anyspace] * 2,
        out_specs=(vmem, vmem),
        scratch_shapes=[
            pltpu.VMEM((count, local, width2), BF16),
            pltpu.SemaphoreType.DMA((len(sizes_in),)),
            pltpu.SemaphoreType.DMA((len(sizes_in),)),
        ],
        compiler_params=params,
        name="gram",
    )(in_hbm(probe), in_hbm(solutions))

    square = jax.ShapeDtypeStruct((order, order), F32)
    tall = jax.ShapeDtypeStruct((3 * order, order), BF16)
    wide = jax.ShapeDtypeStruct((order, 3 * order), BF16)
    stack = jax.ShapeDtypeStruct((2 * count * width, 3 * order), BF16)
    prep = pl.pallas_call(
        functools.partial(prep_kernel, count, blocks),
        out_shape=(
            wide,
            tall,
            tall,
            wide,
            square,
            square,
            square,
            stack,
            jax.ShapeDtypeStruct((count, 6 * order, width2), BF16),
            jax.ShapeDtypeStruct((2 * count * width, order), F32),
        ),
        in_specs=[anyspace] * 4 + [smem, anyspace],
        out_specs=(vmem,) * 10,
        scratch_shapes=[
            pltpu.VMEM((order, order), F32),
            pltpu.VMEM((1, order), F32),
            pltpu.VMEM((order, order), F32),
            pltpu.VMEM((order, order), F32),
            pltpu.SemaphoreType.DMA((4,)),
        ],
        compiler_params=params,
        cost_estimate=pl.CostEstimate(flops=6 * order**3, bytes_accessed=4 << 20, transcendentals=0),
        name="prep",
    )
    turn = pl.pallas_call(
        turn_kernel,
        out_shape=jax.ShapeDtypeStruct((local, width), BF16),
        in_specs=[vmem, anyspace],
        out_specs=vmem,
        compiler_params=params,
        cost_estimate=pl.CostEstimate(flops=0, bytes_accessed=6 << 20, transcendentals=0),
        name="turn",
    )

    def add(terms, after):
        return pl.pallas_call(
            functools.partial(sum_kernel, len(terms)),
            out_shape=summed,
            in_specs=[vmem] * len(terms) + [anyspace] * len(after),
            out_specs=vmem,
            compiler_params=params,
            name="sum",
        )(*terms, *after)

    phases = jnp.asarray(phase_table(total, blocks))
    ready = None
    bits = [1 << k for k in range(1, n_rows.bit_length() - 1)]
    for at in range(0, len(bits), 2):
        step = bits[at : at + 2]
        if len(step) == 2:
            step = [step[0], step[0] ^ step[1], step[1]]
        got = [hop(value, n_pts, n_rows, (0, bit)) for bit in step]
        after = []
        if ready is None:
            factors = (left_factor, singular[None, :], right_factor, adjoint)
            ready = prep(*(in_hbm(v) for v in factors), phases, value)
            after = ready
        value = add([value] + got, after)
    others = [(pts, 0) for pts in range(2, n_pts, 2)]
    if n_rows > 1:
        others = [(1, 1)] + others + [(pts ^ 1, 1) for pts, _ in others]
    grams = [value] + [hop(value, n_pts, n_rows, mask) for mask in others]
    probe_t = turn(held, value)
    rows = (blocks - 1) * width + width // 2
    moments = pl.pallas_call(
        functools.partial(mix_kernel, blocks, [0] + [mask[0] for mask in others]),
        out_shape=jax.ShapeDtypeStruct((rows, width2), F32),
        in_specs=[vmem] * (1 + len(grams)) + [anyspace],
        out_specs=vmem,
        compiler_params=params,
        name="mix",
    )(jnp.asarray(moment_table(total, blocks, width)), *grams, probe_t)
    other = hop(moments, n_pts, n_rows, (1, 0))
    sizes_out = [unit, unit] + [2 * unit] * 7
    return pl.pallas_call(
        functools.partial(post_kernel, sizes_out, blocks),
        out_shape=jax.ShapeDtypeStruct((count, local, width2), BF16),
        in_specs=[vmem] * 13,
        out_specs=anyspace,
        scratch_shapes=[
            pltpu.VMEM((count, local, width2), BF16),
            pltpu.SemaphoreType.DMA((count * len(sizes_out),)),
        ],
        compiler_params=params,
        name="post",
    )(moments, other, *ready, probe_t)


def solution(mesh):
    in_specs = (P("pts", "rows", None), P(None, "rows"), P(), P(), P(), P())
    out_specs = P("pts", "rows", None)
    return jax.shard_map(
        functools.partial(per_device, mesh.shape["pts"], mesh.shape["rows"]),
        mesh=mesh,
        in_specs=in_specs,
        out_specs=out_specs,
        check_vma=False,
    )
```

```python
import functools
import math

import jax
import jax.numpy as jnp
import numpy as np
from jax import lax
from jax.experimental import pallas as pl
from jax.experimental.pallas import tpu as pltpu
from jax.sharding import PartitionSpec as P

F32 = jnp.float32
BF16 = jnp.bfloat16


def dot(first, second):
    return jnp.dot(first, second, preferred_element_type=F32)


def split(value):
    high = value.astype(BF16)
    return high, (value - high.astype(F32)).astype(BF16)


def left3(value):
    high, low = split(value)
    return jnp.concatenate([high, high, low], axis=1)


def right3(value):
    high, low = split(value)
    return jnp.concatenate([high, low, high], axis=0)


def moment_table(total, blocks, width):
    theta = math.pi * (np.arange(total) + 0.5) / total
    table = np.zeros((total, 2 * blocks, 2 * width), np.float32)
    for a in range(blocks):
        left = 2 * a + 2
        right = left + 1 if a < blocks - 1 else left
        cos_l, sin_l = np.cos(left * theta) / total, np.sin(left * theta) / total
        cos_r, sin_r = np.cos(right * theta) / total, np.sin(right * theta) / total
        table[:, a, :width] = cos_l[:, None]
        table[:, a, width:] = -sin_r[:, None]
        table[:, blocks + a, :width] = -sin_l[:, None]
        table[:, blocks + a, width:] = cos_r[:, None]
    return table


def phase_table(total, blocks):
    theta = math.pi * (np.arange(total)[:, None] + 0.5) / total
    half = theta * (np.arange(blocks + 1)[None, :] + 0.5)
    return np.concatenate([np.cos(half), -np.sin(half)], axis=1).astype(np.float32)


def gram_kernel(sizes, probe_hbm, sol_hbm, out_ref, pbuf, sbuf, psem, ssem):
    count = sbuf.shape[0]
    starts = [sum(sizes[:c]) for c in range(len(sizes))]
    step = min(sizes)

    def copies(c):
        at = pl.ds(starts[c], sizes[c])
        return (
            pltpu.make_async_copy(probe_hbm.at[:, at], pbuf.at[:, at], psem.at[c]),
            pltpu.make_async_copy(sol_hbm.at[:, at, :], sbuf.at[:, at, :], ssem.at[c]),
        )

    for c in range(len(sizes)):
        for copy in copies(c):
            copy.start()
    gram = None
    for c in range(len(sizes)):
        for copy in copies(c):
            copy.wait()
        for first in range(starts[c], starts[c] + sizes[c], step):
            at = pl.ds(first, step)
            side = jnp.concatenate([sbuf[p, at, :] for p in range(count)], axis=1)
            part = dot(pbuf[:, at], side)
            gram = part if gram is None else gram + part
    out_ref[...] = gram


def prep_kernel(
    count,
    blocks,
    left_hbm,
    sing_hbm,
    right_hbm,
    adj_hbm,
    phase_ref,
    _,
    ut3_ref,
    w3_ref,
    zt3_ref,
    zl3_ref,
    f1_ref,
    f2_ref,
    dg_ref,
    up3_ref,
    wc3_ref,
    y2_ref,
    left_ref,
    sing_ref,
    right_ref,
    adj_ref,
    sem,
):
    me = lax.axis_index("pts")
    order = left_ref.shape[0]
    fetches = [
        pltpu.make_async_copy(source, held, sem.at[at])
        for at, (source, held) in enumerate(
            [(left_hbm, left_ref), (sing_hbm, sing_ref), (right_hbm, right_ref), (adj_hbm, adj_ref)]
        )
    ]
    for fetch in fetches:
        fetch.start()
    for fetch in fetches:
        fetch.wait()
    width = order // blocks
    left = left_ref[...]
    right = right_ref[...]
    sing = sing_ref[...]
    zbar = adj_ref[...] / sing
    ut3_ref[...] = left3(left.T)
    w3_ref[...] = right3(right)
    zbar_t = zbar.T
    zt3_ref[...] = right3(zbar_t)
    zl3_ref[...] = left3(zbar_t)
    by_column = jnp.broadcast_to(sing, (order, order))
    by_row = by_column.T
    row = lax.broadcasted_iota(jnp.int32, (order, order), 0)
    column = lax.broadcasted_iota(jnp.int32, (order, order), 1)
    eye = row == column
    recip = jnp.where(
        eye, 0.0, 1.0 / jnp.where(eye, 1.0, by_column * by_column - by_row * by_row)
    )
    f1_ref[...] = recip * by_column
    f2_ref[...] = recip * by_row
    dg_ref[...] = jnp.where(eye, -1.0 / by_column, 0.0)
    total = phase_ref.shape[0]
    up, up2 = [], []
    for p in range(count):
        def turn(source, by, sine):
            out = None
            for i in range(blocks):
                term = source[i * width : (i + 1) * width] * phase_ref[
                    me * count + p, sine * (blocks + 1) + by + i
                ]
                out = term if out is None else out + term
            return out

        up += [turn(left, 0, 0) * (1.0 / total), turn(left, 0, 1) * (1.0 / total)]
        up2 += [turn(left, 1, 0) * (1.0 / total), turn(left, 1, 1) * (1.0 / total)]
        wre, wim = turn(right, 0, 0).T, turn(right, 0, 1).T
        wc = jnp.concatenate(
            [jnp.concatenate([wre, wim], axis=1), jnp.concatenate([-wim, wre], axis=1)], axis=0
        )
        wc3_ref[p] = right3(wc)
    up3_ref[...] = left3(jnp.concatenate(up, axis=0))
    y2_ref[...] = dot(left3(jnp.concatenate(up2, axis=0)), right3(zbar))


def sum_kernel(terms, *refs):
    total = refs[0][...]
    for ref in refs[1:terms]:
        total = total + ref[...]
    refs[-1][...] = total


def turn_kernel(probe_ref, _, out_ref):
    out_ref[...] = probe_ref[...].T


def mix_kernel(blocks, masks, table_ref, *refs):
    out_ref = refs[-1]
    width2 = table_ref.shape[2]
    width = width2 // 2
    me = lax.axis_index("pts")
    tiles = [None] * blocks
    for mask, ref in zip(masks, refs[:-1]):
        gram = ref[...]
        count = gram.shape[1] // width2
        for p in range(count):
            straight = gram[:, p * width2 : (p + 1) * width2]
            turned = pltpu.roll(straight, width, 1)
            coef = table_ref[jnp.bitwise_xor(me, mask) * count + p]
            for a in range(blocks):
                term = straight * coef[a : a + 1] + turned * coef[blocks + a : blocks + a + 1]
                tiles[a] = term if tiles[a] is None else tiles[a] + term
    rows = width // 2
    lane = lax.broadcasted_iota(jnp.int32, (rows, width2), 1)
    last = jnp.where(lane < width, tiles[-1][:rows], tiles[-1][rows:])
    out_ref[...] = jnp.concatenate(tiles[:-1] + [last], axis=0)


def hankel_of(moments, blocks):
    width2 = moments.shape[1]
    width = width2 // 2
    tiles = [moments[a * width : (a + 1) * width] for a in range(blocks - 1)]
    packed = moments[(blocks - 1) * width :]
    last = jnp.concatenate([pltpu.roll(packed, width, 1), packed], axis=0)
    lane = lax.broadcasted_iota(jnp.int32, (width, width2), 1)
    turned = [pltpu.roll(tile, width, 1) for tile in tiles] + [last]
    between = [jnp.where(lane < width, turned[a], turned[a + 1]) for a in range(blocks - 1)]
    every = [tile for pair in zip(tiles, between) for tile in pair]
    return jnp.concatenate(
        [
            jnp.concatenate([every[i + j] for j in range(0, blocks, 2)], axis=1)
            for i in range(blocks)
        ],
        axis=0,
    )


def post_kernel(
    sizes,
    blocks,
    own_ref,
    got_ref,
    ut3_ref,
    w3_ref,
    zt3_ref,
    zl3_ref,
    f1_ref,
    f2_ref,
    dg_ref,
    up3_ref,
    wc3_ref,
    y2_ref,
    probe_t_ref,
    out_hbm,
    obuf,
    osem,
):
    count, _, width2 = obuf.shape
    width = width2 // 2
    hankel = hankel_of(own_ref[...] + got_ref[...], blocks)
    quot = dot(ut3_ref[...], right3(hankel))
    zmat = dot(left3(quot), w3_ref[...])
    left_term = dot(left3(zmat), zt3_ref[...])
    right_term = dot(zl3_ref[...], right3(zmat))
    core = right3(
        f1_ref[...] * (left_term - left_term.T)
        + f2_ref[...] * (right_term.T - right_term)
        + dg_ref[...] * right_term
    )
    starts = [sum(sizes[:c]) for c in range(len(sizes))]

    def copy(p, c):
        at = pl.ds(starts[c], sizes[c])
        sem = osem.at[p * len(sizes) + c]
        return pltpu.make_async_copy(obuf.at[p, at, :], out_hbm.at[p, at, :], sem)

    prods = []
    for p in range(count):
        at = pl.ds(2 * p * width, 2 * width)
        prods.append(dot(up3_ref[at, :], core) + y2_ref[at, :])
    for p in range(count):
        pair = jnp.concatenate([prods[p][:width], prods[p][width:]], axis=1)
        weights = dot(left3(pair), wc3_ref[p]).astype(BF16)
        for c in range(len(sizes)):
            at = pl.ds(starts[c], sizes[c])
            obuf[p, at, :] = dot(probe_t_ref[at, :], weights).astype(BF16)
            copy(p, c).start()
    for p in range(count):
        for c in range(len(sizes)):
            copy(p, c).wait()


def hop(value, n_pts, n_rows, mask):
    pairs = [
        (pts * n_rows + row, (pts ^ mask[0]) * n_rows + (row ^ mask[1]))
        for pts in range(n_pts)
        for row in range(n_rows)
    ]
    return lax.ppermute(value, ("pts", "rows"), pairs)


def ring(value, n_pts, n_rows, low, high, step):
    order = [0, low, low | high, high]
    pairs = []
    for pts in range(n_pts):
        for row in range(n_rows):
            rest = row & ~(low | high)
            target = order[(order.index(row & (low | high)) + step) % 4] | rest
            pairs.append((pts * n_rows + row, pts * n_rows + target))
    return lax.ppermute(value, ("pts", "rows"), pairs)


def per_device(n_pts, n_rows, solutions, probe, left_factor, singular, right_factor, adjoint):
    count, local, width2 = solutions.shape
    width = probe.shape[0]
    order = left_factor.shape[0]
    blocks = order // width
    total = count * n_pts
    unit = local // 16
    anyspace = pl.BlockSpec(memory_space=pl.ANY)
    vmem = pl.BlockSpec(memory_space=pltpu.VMEM)
    smem = pl.BlockSpec(memory_space=pltpu.SMEM)
    params = pltpu.CompilerParams(vmem_limit_bytes=20 << 20)
    in_hbm = functools.partial(pltpu.with_memory_space_constraint, memory_space=pltpu.HBM)
    sizes_in = [2 * unit] * 7 + [unit, unit]
    summed = jax.ShapeDtypeStruct((width, count * width2), F32)
    value, held = pl.pallas_call(
        functools.partial(gram_kernel, sizes_in),
        out_shape=(summed, jax.ShapeDtypeStruct((width, local), BF16)),
        in_specs=[anyspace] * 2,
        out_specs=(vmem, vmem),
        scratch_shapes=[
            pltpu.VMEM((count, local, width2), BF16),
            pltpu.SemaphoreType.DMA((len(sizes_in),)),
            pltpu.SemaphoreType.DMA((len(sizes_in),)),
        ],
        compiler_params=params,
        name="gram",
    )(in_hbm(probe), in_hbm(solutions))

    square = jax.ShapeDtypeStruct((order, order), F32)
    tall = jax.ShapeDtypeStruct((3 * order, order), BF16)
    wide = jax.ShapeDtypeStruct((order, 3 * order), BF16)
    stack = jax.ShapeDtypeStruct((2 * count * width, 3 * order), BF16)
    prep = pl.pallas_call(
        functools.partial(prep_kernel, count, blocks),
        out_shape=(
            wide,
            tall,
            tall,
            wide,
            square,
            square,
            square,
            stack,
            jax.ShapeDtypeStruct((count, 6 * order, width2), BF16),
            jax.ShapeDtypeStruct((2 * count * width, order), F32),
        ),
        in_specs=[anyspace] * 4 + [smem, anyspace],
        out_specs=(vmem,) * 10,
        scratch_shapes=[
            pltpu.VMEM((order, order), F32),
            pltpu.VMEM((1, order), F32),
            pltpu.VMEM((order, order), F32),
            pltpu.VMEM((order, order), F32),
            pltpu.SemaphoreType.DMA((4,)),
        ],
        compiler_params=params,
        cost_estimate=pl.CostEstimate(flops=6 * order**3, bytes_accessed=4 << 20, transcendentals=0),
        name="prep",
    )
    turn = pl.pallas_call(
        turn_kernel,
        out_shape=jax.ShapeDtypeStruct((local, width), BF16),
        in_specs=[vmem, anyspace],
        out_specs=vmem,
        compiler_params=params,
        cost_estimate=pl.CostEstimate(flops=0, bytes_accessed=6 << 20, transcendentals=0),
        name="turn",
    )

    def add(terms, after):
        return pl.pallas_call(
            functools.partial(sum_kernel, len(terms)),
            out_shape=summed,
            in_specs=[vmem] * len(terms) + [anyspace] * len(after),
            out_specs=vmem,
            compiler_params=params,
            name="sum",
        )(*terms, *after)

    phases = jnp.asarray(phase_table(total, blocks))
    ready = None
    bits = [1 << k for k in range(1, n_rows.bit_length() - 1)]
    for at in range(0, len(bits), 2):
        step = bits[at : at + 2]
        if len(step) == 2:
            low, high = step
            got = [
                ring(value, n_pts, n_rows, low, high, -1),
                hop(value, n_pts, n_rows, (0, low ^ high)),
                ring(value, n_pts, n_rows, low, high, 1),
            ]
        else:
            got = [hop(value, n_pts, n_rows, (0, step[0]))]
        after = []
        if ready is None:
            factors = (left_factor, singular[None, :], right_factor, adjoint)
            ready = prep(*(in_hbm(v) for v in factors), phases, value)
            after = ready
        value = add([value] + got, after)
    others = [(pts, 0) for pts in range(2, n_pts, 2)]
    if n_rows > 1:
        others = [(1, 1)] + others + [(pts ^ 1, 1) for pts, _ in others]
    grams = [value] + [hop(value, n_pts, n_rows, mask) for mask in others]
    probe_t = turn(held, value)
    rows = (blocks - 1) * width + width // 2
    moments = pl.pallas_call(
        functools.partial(mix_kernel, blocks, [0] + [mask[0] for mask in others]),
        out_shape=jax.ShapeDtypeStruct((rows, width2), F32),
        in_specs=[vmem] * (1 + len(grams)) + [anyspace],
        out_specs=vmem,
        compiler_params=params,
        name="mix",
    )(jnp.asarray(moment_table(total, blocks, width)), *grams, probe_t)
    other = hop(moments, n_pts, n_rows, (1, 0))
    sizes_out = [unit, unit] + [2 * unit] * 7
    return pl.pallas_call(
        functools.partial(post_kernel, sizes_out, blocks),
        out_shape=jax.ShapeDtypeStruct((count, local, width2), BF16),
        in_specs=[vmem] * 13,
        out_specs=anyspace,
        scratch_shapes=[
            pltpu.VMEM((count, local, width2), BF16),
            pltpu.SemaphoreType.DMA((count * len(sizes_out),)),
        ],
        compiler_params=params,
        name="post",
    )(moments, other, *ready, probe_t)


def solution(mesh):
    in_specs = (P("pts", "rows", None), P(None, "rows"), P(), P(), P(), P())
    out_specs = P("pts", "rows", None)
    return jax.shard_map(
        functools.partial(per_device, mesh.shape["pts"], mesh.shape["rows"]),
        mesh=mesh,
        in_specs=in_specs,
        out_specs=out_specs,
        check_vma=False,
    )
```

```python
import functools
import math

import jax
import jax.numpy as jnp
import numpy as np
from jax import lax
from jax.experimental import pallas as pl
from jax.experimental.pallas import tpu as pltpu
from jax.sharding import PartitionSpec as P

F32 = jnp.float32
BF16 = jnp.bfloat16


def dot(first, second):
    return jnp.dot(first, second, preferred_element_type=F32)


def split(value):
    high = value.astype(BF16)
    return high, (value - high.astype(F32)).astype(BF16)


def left3(value):
    high, low = split(value)
    return jnp.concatenate([high, high, low], axis=1)


def right3(value):
    high, low = split(value)
    return jnp.concatenate([high, low, high], axis=0)


def moment_table(total, blocks, width):
    theta = math.pi * (np.arange(total) + 0.5) / total
    table = np.zeros((total, 2 * blocks, 2 * width), np.float32)
    for a in range(blocks):
        left = 2 * a + 2
        right = left + 1 if a < blocks - 1 else left
        cos_l, sin_l = np.cos(left * theta) / total, np.sin(left * theta) / total
        cos_r, sin_r = np.cos(right * theta) / total, np.sin(right * theta) / total
        table[:, a, :width] = cos_l[:, None]
        table[:, a, width:] = -sin_r[:, None]
        table[:, blocks + a, :width] = -sin_l[:, None]
        table[:, blocks + a, width:] = cos_r[:, None]
    return table


def phase_table(total, blocks):
    theta = math.pi * (np.arange(total)[:, None] + 0.5) / total
    half = theta * (np.arange(blocks + 1)[None, :] + 0.5)
    return np.concatenate([np.cos(half), -np.sin(half)], axis=1).astype(np.float32)


def gram_kernel(sizes, probe_hbm, sol_hbm, out_ref, pbuf, sbuf, psem, ssem):
    count = sbuf.shape[0]
    starts = [sum(sizes[:c]) for c in range(len(sizes))]
    step = min(sizes)

    def copies(c):
        at = pl.ds(starts[c], sizes[c])
        return (
            pltpu.make_async_copy(probe_hbm.at[:, at], pbuf.at[:, at], psem.at[c]),
            pltpu.make_async_copy(sol_hbm.at[:, at, :], sbuf.at[:, at, :], ssem.at[c]),
        )

    for c in range(len(sizes)):
        for copy in copies(c):
            copy.start()
    gram = None
    for c in range(len(sizes)):
        for copy in copies(c):
            copy.wait()
        for first in range(starts[c], starts[c] + sizes[c], step):
            at = pl.ds(first, step)
            side = jnp.concatenate([sbuf[p, at, :] for p in range(count)], axis=1)
            part = dot(pbuf[:, at], side)
            gram = part if gram is None else gram + part
    out_ref[...] = gram


def prep_kernel(
    count,
    blocks,
    left_hbm,
    sing_hbm,
    right_hbm,
    adj_hbm,
    phase_ref,
    _,
    ut3_ref,
    w3_ref,
    zt3_ref,
    zl3_ref,
    f1_ref,
    f2_ref,
    dg_ref,
    up3_ref,
    wc3_ref,
    y2_ref,
    left_ref,
    sing_ref,
    right_ref,
    adj_ref,
    sem,
):
    me = lax.axis_index("pts")
    order = left_ref.shape[0]
    fetches = [
        pltpu.make_async_copy(source, held, sem.at[at])
        for at, (source, held) in enumerate(
            [(left_hbm, left_ref), (sing_hbm, sing_ref), (right_hbm, right_ref), (adj_hbm, adj_ref)]
        )
    ]
    for fetch in fetches:
        fetch.start()
    for fetch in fetches:
        fetch.wait()
    width = order // blocks
    left = left_ref[...]
    right = right_ref[...]
    sing = sing_ref[...]
    zbar = adj_ref[...] / sing
    ut3_ref[...] = left3(left.T)
    w3_ref[...] = right3(right)
    zbar_t = zbar.T
    zt3_ref[...] = right3(zbar_t)
    zl3_ref[...] = left3(zbar_t)
    by_column = jnp.broadcast_to(sing, (order, order))
    by_row = by_column.T
    row = lax.broadcasted_iota(jnp.int32, (order, order), 0)
    column = lax.broadcasted_iota(jnp.int32, (order, order), 1)
    eye = row == column
    recip = jnp.where(
        eye, 0.0, 1.0 / jnp.where(eye, 1.0, by_column * by_column - by_row * by_row)
    )
    f1_ref[...] = recip * by_column
    f2_ref[...] = recip * by_row
    dg_ref[...] = jnp.where(eye, -1.0 / by_column, 0.0)
    total = phase_ref.shape[0]
    up, up2 = [], []
    for p in range(count):
        def turn(source, by, sine):
            out = None
            for i in range(blocks):
                term = source[i * width : (i + 1) * width] * phase_ref[
                    me * count + p, sine * (blocks + 1) + by + i
                ]
                out = term if out is None else out + term
            return out

        up += [turn(left, 0, 0) * (1.0 / total), turn(left, 0, 1) * (1.0 / total)]
        up2 += [turn(left, 1, 0) * (1.0 / total), turn(left, 1, 1) * (1.0 / total)]
        wre, wim = turn(right, 0, 0).T, turn(right, 0, 1).T
        wc = jnp.concatenate(
            [jnp.concatenate([wre, wim], axis=1), jnp.concatenate([-wim, wre], axis=1)], axis=0
        )
        wc3_ref[p] = right3(wc)
    up3_ref[...] = left3(jnp.concatenate(up, axis=0))
    y2_ref[...] = dot(left3(jnp.concatenate(up2, axis=0)), right3(zbar))


def sum_kernel(terms, *refs):
    total = refs[0][...]
    for ref in refs[1:terms]:
        total = total + ref[...]
    refs[-1][...] = total


def turn_kernel(probe_ref, _, out_ref):
    out_ref[...] = probe_ref[...].T


def mix_kernel(blocks, masks, table_ref, *refs):
    out_ref = refs[-1]
    width2 = table_ref.shape[2]
    width = width2 // 2
    me = lax.axis_index("pts")
    tiles = [None] * blocks
    for mask, ref in zip(masks, refs[:-1]):
        gram = ref[...]
        count = gram.shape[1] // width2
        for p in range(count):
            straight = gram[:, p * width2 : (p + 1) * width2]
            turned = pltpu.roll(straight, width, 1)
            coef = table_ref[jnp.bitwise_xor(me, mask) * count + p]
            for a in range(blocks):
                term = straight * coef[a : a + 1] + turned * coef[blocks + a : blocks + a + 1]
                tiles[a] = term if tiles[a] is None else tiles[a] + term
    rows = width // 2
    lane = lax.broadcasted_iota(jnp.int32, (rows, width2), 1)
    last = jnp.where(lane < width, tiles[-1][:rows], tiles[-1][rows:])
    out_ref[...] = jnp.concatenate(tiles[:-1] + [last], axis=0)


def hankel_of(moments, blocks):
    width2 = moments.shape[1]
    width = width2 // 2
    tiles = [moments[a * width : (a + 1) * width] for a in range(blocks - 1)]
    packed = moments[(blocks - 1) * width :]
    last = jnp.concatenate([pltpu.roll(packed, width, 1), packed], axis=0)
    lane = lax.broadcasted_iota(jnp.int32, (width, width2), 1)
    turned = [pltpu.roll(tile, width, 1) for tile in tiles] + [last]
    between = [jnp.where(lane < width, turned[a], turned[a + 1]) for a in range(blocks - 1)]
    every = [tile for pair in zip(tiles, between) for tile in pair]
    return jnp.concatenate(
        [
            jnp.concatenate([every[i + j] for j in range(0, blocks, 2)], axis=1)
            for i in range(blocks)
        ],
        axis=0,
    )


def post_kernel(
    sizes,
    blocks,
    own_ref,
    got_ref,
    ut3_ref,
    w3_ref,
    zt3_ref,
    zl3_ref,
    f1_ref,
    f2_ref,
    dg_ref,
    up3_ref,
    wc3_ref,
    y2_ref,
    probe_t_ref,
    out_hbm,
    obuf,
    osem,
):
    count, _, width2 = obuf.shape
    width = width2 // 2
    hankel = hankel_of(own_ref[...] + got_ref[...], blocks)
    quot = dot(ut3_ref[...], right3(hankel))
    zmat = dot(left3(quot), w3_ref[...])
    left_term = dot(left3(zmat), zt3_ref[...])
    right_term = dot(zl3_ref[...], right3(zmat))
    core = right3(
        f1_ref[...] * (left_term - left_term.T)
        + f2_ref[...] * (right_term.T - right_term)
        + dg_ref[...] * right_term
    )
    starts = [sum(sizes[:c]) for c in range(len(sizes))]

    def copy(p, c):
        at = pl.ds(starts[c], sizes[c])
        sem = osem.at[p * len(sizes) + c]
        return pltpu.make_async_copy(obuf.at[p, at, :], out_hbm.at[p, at, :], sem)

    prods = []
    for p in range(count):
        at = pl.ds(2 * p * width, 2 * width)
        prods.append(dot(up3_ref[at, :], core) + y2_ref[at, :])
    for p in range(count):
        pair = jnp.concatenate([prods[p][:width], prods[p][width:]], axis=1)
        weights = dot(left3(pair), wc3_ref[p]).astype(BF16)
        for c in range(len(sizes)):
            at = pl.ds(starts[c], sizes[c])
            obuf[p, at, :] = dot(probe_t_ref[at, :], weights).astype(BF16)
            copy(p, c).start()
    for p in range(count):
        for c in range(len(sizes)):
            copy(p, c).wait()


def hop(value, n_pts, n_rows, mask):
    pairs = [
        (pts * n_rows + row, (pts ^ mask[0]) * n_rows + (row ^ mask[1]))
        for pts in range(n_pts)
        for row in range(n_rows)
    ]
    return lax.ppermute(value, ("pts", "rows"), pairs)


def ring(value, n_pts, n_rows, low, high, step):
    order = [0, low, low | high, high]
    pairs = []
    for pts in range(n_pts):
        for row in range(n_rows):
            rest = row & ~(low | high)
            target = order[(order.index(row & (low | high)) + step) % 4] | rest
            pairs.append((pts * n_rows + row, pts * n_rows + target))
    return lax.ppermute(value, ("pts", "rows"), pairs)


def per_device(n_pts, n_rows, solutions, probe, left_factor, singular, right_factor, adjoint):
    count, local, width2 = solutions.shape
    width = probe.shape[0]
    order = left_factor.shape[0]
    blocks = order // width
    total = count * n_pts
    unit = local // 16
    anyspace = pl.BlockSpec(memory_space=pl.ANY)
    vmem = pl.BlockSpec(memory_space=pltpu.VMEM)
    smem = pl.BlockSpec(memory_space=pltpu.SMEM)
    params = pltpu.CompilerParams(vmem_limit_bytes=20 << 20)
    in_hbm = functools.partial(pltpu.with_memory_space_constraint, memory_space=pltpu.HBM)
    sizes_in = [2 * unit] * 7 + [unit, unit]
    summed = jax.ShapeDtypeStruct((width, count * width2), F32)
    value, held = pl.pallas_call(
        functools.partial(gram_kernel, sizes_in),
        out_shape=(summed, jax.ShapeDtypeStruct((width, local), BF16)),
        in_specs=[anyspace] * 2,
        out_specs=(vmem, vmem),
        scratch_shapes=[
            pltpu.VMEM((count, local, width2), BF16),
            pltpu.SemaphoreType.DMA((len(sizes_in),)),
            pltpu.SemaphoreType.DMA((len(sizes_in),)),
        ],
        compiler_params=params,
        name="gram",
    )(in_hbm(probe), in_hbm(solutions))

    square = jax.ShapeDtypeStruct((order, order), F32)
    tall = jax.ShapeDtypeStruct((3 * order, order), BF16)
    wide = jax.ShapeDtypeStruct((order, 3 * order), BF16)
    stack = jax.ShapeDtypeStruct((2 * count * width, 3 * order), BF16)
    prep = pl.pallas_call(
        functools.partial(prep_kernel, count, blocks),
        out_shape=(
            wide,
            tall,
            tall,
            wide,
            square,
            square,
            square,
            stack,
            jax.ShapeDtypeStruct((count, 6 * order, width2), BF16),
            jax.ShapeDtypeStruct((2 * count * width, order), F32),
        ),
        in_specs=[anyspace] * 4 + [smem, anyspace],
        out_specs=(vmem,) * 10,
        scratch_shapes=[
            pltpu.VMEM((order, order), F32),
            pltpu.VMEM((1, order), F32),
            pltpu.VMEM((order, order), F32),
            pltpu.VMEM((order, order), F32),
            pltpu.SemaphoreType.DMA((4,)),
        ],
        compiler_params=params,
        cost_estimate=pl.CostEstimate(flops=6 * order**3, bytes_accessed=4 << 20, transcendentals=0),
        name="prep",
    )
    turn = pl.pallas_call(
        turn_kernel,
        out_shape=jax.ShapeDtypeStruct((local, width), BF16),
        in_specs=[vmem, anyspace],
        out_specs=vmem,
        compiler_params=params,
        cost_estimate=pl.CostEstimate(flops=0, bytes_accessed=6 << 20, transcendentals=0),
        name="turn",
    )

    def add(terms, after):
        return pl.pallas_call(
            functools.partial(sum_kernel, len(terms)),
            out_shape=summed,
            in_specs=[vmem] * len(terms) + [anyspace] * len(after),
            out_specs=vmem,
            compiler_params=params,
            name="sum",
        )(*terms, *after)

    phases = jnp.asarray(phase_table(total, blocks))
    ready = None
    bits = [1 << k for k in range(1, n_rows.bit_length() - 1)]
    for at in range(0, len(bits), 2):
        step = bits[at : at + 2]
        if len(step) == 2:
            low, high = step
            got = [
                ring(value, n_pts, n_rows, low, high, -1),
                hop(value, n_pts, n_rows, (0, low ^ high)),
                ring(value, n_pts, n_rows, low, high, 1),
            ]
        else:
            got = [hop(value, n_pts, n_rows, (0, step[0]))]
        after = []
        if ready is None:
            factors = (left_factor, singular[None, :], right_factor, adjoint)
            ready = prep(*(in_hbm(v) for v in factors), phases, value)
            probe_t = turn(held, value)
            after = [*ready, probe_t]
        value = add([value] + got, after)
    others = [(pts, 0) for pts in range(2, n_pts, 2)]
    if n_rows > 1:
        others = [(1, 1)] + others + [(pts ^ 1, 1) for pts, _ in others]
    grams = [value] + [hop(value, n_pts, n_rows, mask) for mask in others]
    rows = (blocks - 1) * width + width // 2
    moments = pl.pallas_call(
        functools.partial(mix_kernel, blocks, [0] + [mask[0] for mask in others]),
        out_shape=jax.ShapeDtypeStruct((rows, width2), F32),
        in_specs=[vmem] * (1 + len(grams)),
        out_specs=vmem,
        compiler_params=params,
        name="mix",
    )(jnp.asarray(moment_table(total, blocks, width)), *grams)
    other = hop(moments, n_pts, n_rows, (1, 0))
    sizes_out = [unit, unit] + [2 * unit] * 7
    return pl.pallas_call(
        functools.partial(post_kernel, sizes_out, blocks),
        out_shape=jax.ShapeDtypeStruct((count, local, width2), BF16),
        in_specs=[vmem] * 13,
        out_specs=anyspace,
        scratch_shapes=[
            pltpu.VMEM((count, local, width2), BF16),
            pltpu.SemaphoreType.DMA((count * len(sizes_out),)),
        ],
        compiler_params=params,
        name="post",
    )(moments, other, *ready, probe_t)


def solution(mesh):
    in_specs = (P("pts", "rows", None), P(None, "rows"), P(), P(), P(), P())
    out_specs = P("pts", "rows", None)
    return jax.shard_map(
        functools.partial(per_device, mesh.shape["pts"], mesh.shape["rows"]),
        mesh=mesh,
        in_specs=in_specs,
        out_specs=out_specs,
        check_vma=False,
    )
```
